256 devices in a mesh: pair: 64 (over z_hi, y, x, core), sec: 4 (over z_lo).
Axes of the slice: x: 4, y: 4, z: 8 (z_hi: 2, z_lo: 4; z = z_hi * 4 + z_lo), core: 2. Of those that a mesh axis runs over, the one named last changes fastest.
Arguments:
- normal_ops: float32 [2, 128, 128, 512], P(None, 'pair', None, 'sec'), may hold values from -6 to 6
- integrals: float32 [2, 64, 128], P(None, 'pair'), may hold values from -1.5 to 1.5
- site_terms: float32 [2, 64, 4, 4], P(None, 'pair'), may hold values from -8 to 8
- basis: float32 [2, 4, 512, 512], P(None, None, None, 'sec'), may hold values from -0.25 to 0.25
Outputs:
- new_normal: float32 [2, 128, 4, 128, 512], P(None, 'pair', None, None, 'sec')
- new_comp: float32 [2, 64, 4, 128, 512], P(None, 'pair', None, None, 'sec')
The draws below stay inside these ranges and needn't reach their ends.
All inputs are finite; a program needn't handle non-finite values.
Results may differ from the reference program's by a relative error of at most 0.00007.
Values sent between devices are 32-bit elements; how exact they have to be, the bound alone decides.
A program may use at most 64 MiB of HBM per device.

```python
import jax
import jax.numpy as jnp
from jax import lax

SDIM = 512
SITE = 4
ROWS = 128
NORM = 128
COMP = 64


def strengthened(drawn, rng, source, target, blocks, factor):
    owner, partner = [(jnp.arange(drawn.shape[position]) // (drawn.shape[position] // blocks)).reshape([-1 if axis == position else 1 for axis in range(drawn.ndim)]) for position in (source, target)]
    chosen = jax.random.permutation(rng, blocks)[partner]
    strong = (owner == chosen) | (owner == (partner + blocks // 2) % blocks)
    return jnp.where(strong, factor * drawn, drawn)


def block_levels(rng, extent, shards, least, largest):
    def one(axis_at, parts):
        heights = jax.random.uniform(jax.random.fold_in(jax.random.fold_in(rng, 6), axis_at), (parts,), jnp.float32, least / len(shards), largest / len(shards))
        return jnp.repeat(jnp.exp(heights), extent[axis_at] // parts).reshape((-1,) + (1,) * (len(extent) - axis_at - 1))

    loudness = one(*shards[0])
    for cut in shards[1:]:
        loudness = loudness * one(*cut)
    return loudness


def scatter_about(stream_key, shape, spread, limit, pieces=(), held_as=jnp.bfloat16):
    values = spread * jax.random.normal(stream_key, shape, jnp.float32)
    if pieces:
        values = values * block_levels(stream_key, shape, pieces, -0.22, 0.18)
    return jnp.clip(values, -limit, limit).astype(held_as)


def heavy_noise(key, dims, scale, most, pieces, heavy, kind=jnp.bfloat16):
    array = scale * jax.random.normal(key, dims, jnp.float32)
    if pieces:
        array = array * block_levels(key, dims, pieces, -0.22, 0.18)
    return jnp.clip(strengthened(array, jax.random.fold_in(key, 3), *heavy), -most, most).astype(kind)


def setup_inputs(seed: int = 0) -> dict:
    arg_keys = jax.random.split(jax.random.key(seed), 5)
    normal_ops = scatter_about(arg_keys[0], (2, NORM, ROWS, SDIM), 1.0, 6.0, ((1, 64), (3, 4)), jnp.float32)
    integrals = heavy_noise(arg_keys[1], (2, COMP, NORM), NORM ** -0.5, 1.5, ((1, 64),), (2, 1, 64, 4.0), jnp.float32)
    site_terms = scatter_about(arg_keys[2], (2, COMP, SITE, SITE), 2.0, 8.0, ((1, 64),), jnp.float32)
    basis = scatter_about(arg_keys[3], (2, SITE, SDIM, SDIM), SDIM ** -0.5, 0.25, ((3, 4),), jnp.float32)
    return {"normal_ops": normal_ops, "integrals": integrals, "site_terms": site_terms, "basis": basis}


highest = lax.Precision.HIGHEST


def complex_einsum(form, left, right):
    real_part = jnp.einsum(form, left[0], right[0], precision=highest) - jnp.einsum(form, left[1], right[1], precision=highest)
    imag_part = jnp.einsum(form, left[0], right[1], precision=highest) + jnp.einsum(form, left[1], right[0], precision=highest)
    return jnp.stack([real_part, imag_part])


def reference(normal_ops, integrals, site_terms, basis):
    comp_ops = complex_einsum("pr,rxc->pxc", integrals, normal_ops)
    row_count = normal_ops.shape[2]

    def renorm_one(operator):
        return complex_einsum("ij,ajn->ain", operator, basis)

    new_normal = lax.map(renorm_one, jnp.transpose(normal_ops, (1, 0, 2, 3)))
    new_normal = jnp.transpose(new_normal, (1, 0, 2, 3, 4))
    new_comp = lax.map(renorm_one, jnp.transpose(comp_ops, (1, 0, 2, 3)))
    new_comp = jnp.transpose(new_comp, (1, 0, 2, 3, 4))
    site_part = complex_einsum("pab,bin->pain", site_terms, basis[:, :, :row_count, :])
    return new_normal, new_comp + site_part
```

```python
import jax
import jax.numpy as jnp
from jax import lax
from jax.experimental import pallas as pl
from jax.experimental.pallas import tpu as pltpu
from jax.sharding import PartitionSpec as P

MESH = pl.DeviceIdType.MESH
F32 = jnp.float32
BF16 = jnp.bfloat16
RIGHT, LEFT = 0, 1


def split(x):
    high = x.astype(BF16)
    return high, (x - high.astype(F32)).astype(BF16)


def kernel(
    n_ref, i_ref, t_ref, b_hbm, on_ref, oc_ref,
    bas, bhi, blo, nall, rows, coef, part, done, ochain, xchain,
    b_sem, n_s, n_r, f_s, f_r, c_s, c_r, iz_s, iz_r, ip_s, ip_r, k_s, k_r, o_s, o_r, x_s, x_r,
):
    p = lax.axis_index("pair")
    s = lax.axis_index("sec")
    half = p // 32
    chip = (p // 2) % 16
    core = p % 2
    pairing = s // 2
    odd = s % 2

    def on_chip(q):
        return (half * 32 + q * 2 + core, s)

    mate = (p - core + (1 - core), s)
    z_up = ((p + 32 * ((s + 1) // 4)) % 64, (s + 1) % 4)
    z_down = ((p + 32 * ((4 - s) // 4)) % 64, (s + 3) % 4)
    z_to = (z_up, z_down)

    def remote(src, dst, send, recv, to):
        return pltpu.make_async_remote_copy(
            src_ref=src, dst_ref=dst, send_sem=send, recv_sem=recv, device_id=to, device_id_type=MESH
        )

    def wait_for(ref, sem):
        pltpu.make_async_copy(ref, ref, sem).wait()

    basis_copy = pltpu.make_async_copy(b_hbm, bas, b_sem)
    basis_copy.start()

    re = jnp.broadcast_to(i_ref[0], (8, 128))
    im = jnp.broadcast_to(i_ref[1], (8, 128))
    re_t, im_t = pltpu.roll(re, 64, 1), pltpu.roll(im, 64, 1)
    low = lax.broadcasted_iota(jnp.int32, (8, 128), 1) < 64
    row = lax.broadcasted_iota(jnp.int32, (8, 128), 0)
    tile = jnp.where(
        row == 0,
        jnp.where(low, re, -im_t),
        jnp.where(
            row == 1,
            jnp.where(low, im, re_t),
            jnp.where(row == 2, jnp.where(low, re_t, -im), jnp.where(low, im_t, re)),
        ),
    )
    coef[half, chip] = tile

    barrier = pltpu.get_barrier_semaphore()

    @pl.loop(1, 16)
    def _(d):
        pl.semaphore_signal(barrier, inc=1, device_id=on_chip((chip + d) % 16), device_id_type=MESH)

    for to in (mate, z_up, z_down):
        pl.semaphore_signal(barrier, inc=1, device_id=to, device_id_type=MESH)
    pl.semaphore_wait(barrier, 18)

    def n_slot(way, k):
        return s - k if way == RIGHT else s + k

    def n_can_send(way, k):
        return (s < 3) & (s >= k) if way == RIGHT else (s > 0) & (s + k <= 3)

    def n_can_recv(way, k):
        return s - 1 >= k if way == RIGHT else s + 1 + k <= 3

    def n_copy(way, k, ch):
        slot = n_slot(way, k)
        src = n_ref.at[ch] if k == 0 else nall.at[slot, ch]
        return remote(src, nall.at[slot, ch], n_s.at[way, k, ch], n_r.at[way, k, ch], z_to[way])

    def n_send(way, k, ch):
        @pl.when(n_can_send(way, k))
        def _():
            n_copy(way, k, ch).start()

    def n_wait(way, k, ch):
        @pl.when(n_can_recv(way, k))
        def _():
            wait_for(nall.at[n_slot(way, k + 1), ch], n_r.at[way, k, ch])

    for ch in range(2):
        for way in (RIGHT, LEFT):
            n_send(way, 0, ch)

    def forward(inv, src):
        @pl.loop(1, 16)
        def _(d):
            q = (chip + d) % 16
            remote(src.at[:, :, q], rows.at[inv, :, chip, core], f_s.at[inv], f_r.at[inv], on_chip(q)).start()

        rows[inv, :, chip, core] = src[:, :, chip]

    forward(0, n_ref)

    @pl.when(s == 3)
    def _():
        remote(coef.at[half, chip], coef.at[half, chip], iz_s, iz_r, z_up).start()

    @pl.when(s == 0)
    def _():
        remote(coef.at[half, chip], coef.at[half, chip], iz_s, iz_r, z_down).start()

    basis_copy.wait()
    for g in range(4):
        for r in range(2):
            for a in range(4):
                high, rest = split(bas[r, a, pl.ds(128 * g, 128)])
                bhi[g, pl.ds(128 * r, 128), pl.ds(128 * a, 128)] = high
                blo[g, pl.ds(128 * r, 128), pl.ds(128 * a, 128)] = rest

    wait_for(coef.at[1 - half, chip], iz_r)

    @pl.when(s == 0)
    def _():
        remote(coef.at[1 - half, chip], coef.at[1 - half, chip], iz_s, iz_r, z_up).start()

    @pl.when(s == 3)
    def _():
        remote(coef.at[1 - half, chip], coef.at[1 - half, chip], iz_s, iz_r, z_down).start()

    @pl.loop(1, 16)
    def _(d):
        remote(coef.at[:, chip], coef.at[:, chip], ip_s, ip_r, on_chip((chip + d) % 16)).start()

    def product(real, imag, g):
        top = split(jnp.concatenate([real, -imag], axis=1))
        bottom = split(jnp.concatenate([imag, real], axis=1))
        out = []
        for high, rest in (top, bottom):
            for pair in range(2):
                cols = pl.ds(256 * pair, 256)
                b_high, b_rest = bhi[g, :, cols], blo[g, :, cols]
                dot = lambda x, y: jnp.dot(x, y, preferred_element_type=F32)
                out.append(dot(high, b_high) + (dot(high, b_rest) + dot(rest, b_high)))
        return out

    def renorm_normal(src, g, first=False):
        for j in range(2):
            real = src[0, j].reshape(128, 128)
            imag = src[1, j].reshape(128, 128)
            res = product(real, imag, g)
            for r in range(2):
                for a in range(4):
                    value = res[2 * r + a // 2][:, 128 * (a % 2) : 128 * (a % 2) + 128]
                    if first:
                        on_ref[r, j, a] = value
                    else:
                        on_ref[r, j, a] += value

    def renorm_comp(real, imag, g):
        res = product(real.reshape(128, 128), imag.reshape(128, 128), g)
        for r in range(2):
            for a in range(4):
                oc_ref[r, 0, a] += res[2 * r + a // 2][:, 128 * (a % 2) : 128 * (a % 2) + 128]

    renorm_normal(n_ref, s, first=True)

    for a in range(4):
        real = jnp.zeros((128, 128), F32)
        imag = jnp.zeros((128, 128), F32)
        for b in range(4):
            t_re, t_im = t_ref[0, 0, a, b], t_ref[1, 0, a, b]
            b_re, b_im = bas[0, b, pl.ds(0, 128)], bas[1, b, pl.ds(0, 128)]
            real += t_re * b_re - t_im * b_im
            imag += t_re * b_im + t_im * b_re
        oc_ref[0, 0, a] = real
        oc_ref[1, 0, a] = imag

    def swap(inv):
        wait_for(rows.at[inv, :, pl.ds(0, 15), 0], f_r.at[inv])
        remote(rows.at[inv, :, :, core], rows.at[inv, :, :, core], c_s.at[inv], c_r.at[inv], mate).start()

    def complementary(inv):
        wait_for(rows.at[inv, :, :, 1 - core], c_r.at[inv])
        flat = rows.at[inv].reshape(1024, 128)
        table = coef.reshape(256, 128)
        lines = [table[pl.ds(i, 32, stride=8), :] for i in range(4)]
        left = jnp.concatenate(
            [jnp.where(half == 0, lines[0], lines[2]), jnp.where(half == 0, lines[1], lines[3])], axis=0
        )
        out = part.at[inv].reshape(512, 128)
        for i in range(8):
            res = jnp.dot(left, flat[pl.ds(i, 128, stride=8), :], preferred_element_type=F32, precision=lax.Precision.HIGHEST)
            out[pl.ds(i, 64, stride=8), :] = res

    def back(inv, gi):
        @pl.loop(1, 16)
        def _(d):
            q = (chip + d) % 16
            remote(part.at[inv, :, :, q], done.at[gi, :, :, chip], k_s.at[inv], k_r.at[inv], on_chip(q)).start()

        done[gi, :, :, chip] = part[inv, :, :, chip]

    def wait_back(inv, gi):
        wait_for(done.at[gi, :, :, pl.ds(0, 15)], k_r.at[inv])

    def x_group(way, t):
        return 3 - t if way == RIGHT else t

    def x_copy(way, t, ch, origin):
        g = x_group(way, t)
        src = done.at[g % 2, ch, 1 - half] if origin else xchain.at[g, ch]
        return remote(src, xchain.at[g, ch], x_s.at[way, t, ch], x_r.at[way, t, ch], z_to[way])

    def o_copy(way, t, ch, origin):
        gi = 1 - t if way == RIGHT else t
        src = done.at[gi, ch, half] if origin else ochain.at[gi, ch]
        return remote(src, ochain.at[gi, ch], o_s.at[way, t, ch], o_r.at[t, ch], z_to[way])

    def originate(t):
        for ch in range(2):
            @pl.when(s == 3)
            def _():
                x_copy(RIGHT, t, ch, True).start()

            @pl.when(s == 0)
            def _():
                x_copy(LEFT, t, ch, True).start()

            @pl.when(s == 1)
            def _():
                o_copy(RIGHT, t, ch, True).start()

            @pl.when(s == 2)
            def _():
                o_copy(LEFT, t, ch, True).start()

    def x_take(way, t, ch):
        wait_for(xchain.at[x_group(way, t), ch], x_r.at[way, t, ch])

        @pl.when(s < 3 if way == RIGHT else s > 0)
        def _():
            x_copy(way, t, ch, False).start()

    def o_take(t, ch):
        @pl.when(s < 2)
        def _():
            wait_for(ochain.at[t, ch], o_r.at[t, ch])

            @pl.when(s == 1)
            def _():
                o_copy(LEFT, t, ch, False).start()

        @pl.when(s >= 2)
        def _():
            wait_for(ochain.at[1 - t, ch], o_r.at[t, ch])

            @pl.when(s == 2)
            def _():
                o_copy(RIGHT, t, ch, False).start()

    def near(t):
        for ch in range(2):
            @pl.when(s < 2)
            def _():
                x_take(RIGHT, t, ch)

            @pl.when(s >= 2)
            def _():
                x_take(LEFT, t, ch)

    def far(t):
        for ch in range(2):
            @pl.when(s < 2)
            def _():
                x_take(LEFT, t, ch)

            @pl.when(s >= 2)
            def _():
                x_take(RIGHT, t, ch)

    def n_step(k):
        for ch in range(2):
            for way in (RIGHT, LEFT):
                n_wait(way, k, ch)
                if k < 2:
                    n_send(way, k + 1, ch)

    def n_renorm(k):
        for way in (RIGHT, LEFT):
            @pl.when(n_can_recv(way, k))
            def _():
                slot = n_slot(way, k + 1)
                renorm_normal(nall.at[slot], slot)

    other = s + 1 - 2 * odd
    swap(0)
    n_step(0)
    forward(1, nall.at[other])
    wait_for(coef.at[:, pl.ds(0, 15)], ip_r)
    complementary(0)
    back(0, odd)
    n_renorm(0)
    swap(1)
    n_step(1)
    wait_back(0, odd)
    originate(0)
    complementary(1)
    back(1, 1 - odd)
    n_renorm(1)
    near(0)
    for ch in range(2):
        o_take(0, ch)
    n_step(2)
    wait_back(1, 1 - odd)
    originate(1)
    n_renorm(2)
    far(0)
    near(1)
    for ch in range(2):
        o_take(1, ch)
    far(1)
    for gi in range(2):
        g = 2 * pairing + gi
        renorm_comp(done[gi, 0, half] + xchain[g, 0], done[gi, 1, half] + xchain[g, 1], g)
        g = 2 * (1 - pairing) + gi
        renorm_comp(ochain[gi, 0] + xchain[g, 0], ochain[gi, 1] + xchain[g, 1], g)

    for ch in range(2):
        for way in (RIGHT, LEFT):
            for k in range(3):
                @pl.when(n_can_send(way, k))
                def _():
                    wait_for(nall.at[0, ch], n_s.at[way, k, ch])

            for t in range(2):
                wait_for(xchain.at[0, ch], x_s.at[way, t, ch])

        for t in range(2):
            @pl.when((s == 1) | (s == 2))
            def _():
                wait_for(ochain.at[0, ch], o_s.at[RIGHT, t, ch])
                wait_for(ochain.at[0, ch], o_s.at[LEFT, t, ch])

    for inv in range(2):
        wait_for(rows.at[inv, :, pl.ds(0, 15), 0], f_s.at[inv])
        wait_for(rows.at[inv, :, :, core], c_s.at[inv])
        wait_for(part.at[inv, :, :, pl.ds(0, 15)], k_s.at[inv])
    wait_for(coef.at[:, pl.ds(0, 15)], ip_s)

    @pl.when((s == 0) | (s == 3))
    def _():
        wait_for(coef.at[:, 0], iz_s)


def on_device(normal_ops, integrals, site_terms, basis):
    sem = pltpu.SemaphoreType.DMA
    vmem = pl.BlockSpec(memory_space=pltpu.VMEM)
    return pl.pallas_call(
        kernel,
        name="renormalize",
        out_shape=(
            jax.ShapeDtypeStruct((2, 2, 4, 128, 128), F32),
            jax.ShapeDtypeStruct((2, 1, 4, 128, 128), F32),
        ),
        in_specs=[vmem, vmem, pl.BlockSpec(memory_space=pltpu.SMEM), pl.BlockSpec(memory_space=pl.ANY)],
        out_specs=(vmem, vmem),
        scratch_shapes=[
            pltpu.VMEM((2, 4, 512, 128), F32),
            pltpu.VMEM((4, 256, 512), BF16),
            pltpu.VMEM((4, 256, 512), BF16),
            pltpu.VMEM((4, 2, 2, 16, 8, 128), F32),
            pltpu.VMEM((2, 2, 16, 2, 2, 8, 128), F32),
            pltpu.VMEM((2, 16, 8, 128), F32),
            pltpu.VMEM((2, 2, 2, 16, 8, 128), F32),
            pltpu.VMEM((2, 2, 2, 16, 8, 128), F32),
            pltpu.VMEM((2, 2, 16, 8, 128), F32),
            pltpu.VMEM((4, 2, 16, 8, 128), F32),
            sem,
            sem((2, 3, 2)), sem((2, 3, 2)),
            sem((2,)), sem((2,)),
            sem((2,)), sem((2,)),
            sem, sem, sem, sem,
            sem((2,)), sem((2,)),
            sem((2, 2, 2)), sem((2, 2)),
            sem((2, 2, 2)), sem((2, 2, 2)),
        ],
        compiler_params=pltpu.CompilerParams(
            collective_id=0, has_side_effects=True, vmem_limit_bytes=32 * 2**20
        ),
    )(normal_ops.reshape(2, 2, 16, 8, 128), integrals, site_terms, basis)


def solution(mesh):
    placed = (
        P(None, "pair", None, "sec"),
        P(None, "pair", None),
        P(None, "pair", None, None),
        P(None, None, None, "sec"),
    )
    return jax.shard_map(
        on_device,
        mesh=mesh,
        in_specs=placed,
        out_specs=(P(None, "pair", None, None, "sec"), P(None, "pair", None, None, "sec")),
        check_vma=False,
    )
```

```python
import jax
import jax.numpy as jnp
from jax import lax
from jax.experimental import pallas as pl
from jax.experimental.pallas import tpu as pltpu
from jax.sharding import PartitionSpec as P

MESH = pl.DeviceIdType.MESH
F32 = jnp.float32
BF16 = jnp.bfloat16
RIGHT, LEFT = 0, 1


def split(x):
    high = x.astype(BF16)
    return high, (x - high.astype(F32)).astype(BF16)


def kernel(
    n_hbm, i_hbm, t_hbm, b_hbm, on_ref, oc_ref,
    i_ref, t_ref, bas, bhi, blo, nall, rows, coef, part, done, ochain, xchain,
    in_sem, n_s, n_r, f_s, f_r, c_s, c_r, iz_s, iz_r, ip_s, ip_r, k_s, k_r, oo_s, of_s, o_r, xo_s, xf_s, x_r,
):
    p = lax.axis_index("pair")
    s = lax.axis_index("sec")
    half = p // 32
    chip = (p // 2) % 16
    core = p % 2
    pairing = s // 2
    odd = s % 2

    def on_chip(q):
        return (half * 32 + q * 2 + core, s)

    mate = (p - core + (1 - core), s)
    z_up = ((p + 32 * ((s + 1) // 4)) % 64, (s + 1) % 4)
    z_down = ((p + 32 * ((4 - s) // 4)) % 64, (s + 3) % 4)
    z_to = (z_up, z_down)
    edge = (s == 0) | (s == 3)
    edge_beyond = ((p + 32) % 64, 3 * (s // 2))
    inner_beyond = ((p + 32) % 64, 1 + s // 2)

    def remote(src, dst, send, recv, to):
        return pltpu.make_async_remote_copy(
            src_ref=src, dst_ref=dst, send_sem=send, recv_sem=recv, device_id=to, device_id_type=MESH
        )

    def wait_for(ref, sem):
        pltpu.make_async_copy(ref, ref, sem).wait()

    copies = [
        pltpu.make_async_copy(src, dst, in_sem.at[k])
        for k, (src, dst) in enumerate(((i_hbm, i_ref), (n_hbm, nall.at[s]), (t_hbm, t_ref), (b_hbm, bas)))
    ]
    for copy in copies:
        copy.start()

    barrier = pltpu.get_barrier_semaphore()

    @pl.loop(1, 16)
    def _(d):
        pl.semaphore_signal(barrier, inc=1, device_id=on_chip((chip + d) % 16), device_id_type=MESH)

    for to in (mate, z_up, z_down):
        pl.semaphore_signal(barrier, inc=1, device_id=to, device_id_type=MESH)

    @pl.when(edge)
    def _():
        pl.semaphore_signal(barrier, inc=1, device_id=inner_beyond, device_id_type=MESH)

    copies[0].wait()
    re = jnp.broadcast_to(i_ref[0], (8, 128))
    im = jnp.broadcast_to(i_ref[1], (8, 128))
    re_t, im_t = pltpu.roll(re, 64, 1), pltpu.roll(im, 64, 1)
    low = lax.broadcasted_iota(jnp.int32, (8, 128), 1) < 64
    row = lax.broadcasted_iota(jnp.int32, (8, 128), 0)
    tile = jnp.where(
        row == 0,
        jnp.where(low, re, -im_t),
        jnp.where(
            row == 1,
            jnp.where(low, im, re_t),
            jnp.where(row == 2, jnp.where(low, re_t, -im), jnp.where(low, im_t, re)),
        ),
    )
    coef[half, chip] = tile
    copies[1].wait()
    pl.semaphore_wait(barrier, jnp.where(edge, 18, 19))


    @pl.when(s == 3)
    def _():
        remote(coef.at[half, chip], coef.at[half, chip], iz_s, iz_r, z_up).start()

    @pl.when(s == 0)
    def _():
        remote(coef.at[half, chip], coef.at[half, chip], iz_s, iz_r, z_down).start()

    def n_slot(way, k):
        return s - k if way == RIGHT else s + k

    def n_can_send(way, k):
        return (s < 3) & (s >= k) if way == RIGHT else (s > 0) & (s + k <= 3)

    def n_can_recv(way, k):
        return s - 1 >= k if way == RIGHT else s + 1 + k <= 3

    def n_piece(slot, c):
        return nall.at[slot, c // 2, c % 2]

    def n_send(way, k, c):
        @pl.when(n_can_send(way, k))
        def _():
            piece = n_piece(n_slot(way, k), c)
            remote(piece, piece, n_s.at[way, k, c], n_r.at[way, k, c], z_to[way]).start()

    def n_wait(way, k, c):
        @pl.when(n_can_recv(way, k))
        def _():
            wait_for(n_piece(n_slot(way, k + 1), c), n_r.at[way, k, c])

    for c in range(4):
        for way in (RIGHT, LEFT):
            n_send(way, 0, c)

    def forward(inv, slot, r):
        @pl.loop(1, 16)
        def _(d):
            q = (chip + d) % 16
            remote(nall.at[slot, r, :, q], rows.at[inv, r, chip, core], f_s.at[inv], f_r.at[inv], on_chip(q)).start()

        rows[inv, r, chip, core] = nall[slot, r, :, chip]

    def forward_whole(inv, slot):
        @pl.loop(1, 16)
        def _(d):
            q = (chip + d) % 16
            remote(nall.at[slot, :, :, q], rows.at[inv, :, chip, core], f_s.at[inv], f_r.at[inv], on_chip(q)).start()

        rows[inv, :, chip, core] = nall[slot, :, :, chip]

    forward_whole(0, s)

    wait_for(coef.at[1 - half, chip], iz_r)

    @pl.when(s == 0)
    def _():
        remote(coef.at[1 - half, chip], coef.at[1 - half, chip], iz_s, iz_r, z_up).start()

    @pl.when(s == 3)
    def _():
        remote(coef.at[1 - half, chip], coef.at[1 - half, chip], iz_s, iz_r, z_down).start()

    @pl.loop(1, 16)
    def _(d):
        remote(coef.at[:, chip], coef.at[:, chip], ip_s, ip_r, on_chip((chip + d) % 16)).start()

    copies[3].wait()
    for g in range(4):
        for r in range(2):
            for a in range(4):
                high, rest = split(bas[r, a, pl.ds(128 * g, 128)])
                bhi[g, pl.ds(128 * r, 128), pl.ds(128 * a, 128)] = high
                blo[g, pl.ds(128 * r, 128), pl.ds(128 * a, 128)] = rest

    def product(real, imag, g):
        top = split(jnp.concatenate([real, -imag], axis=1))
        bottom = split(jnp.concatenate([imag, real], axis=1))
        out = []
        for high, rest in (top, bottom):
            for pair in range(2):
                cols = pl.ds(256 * pair, 256)
                b_high, b_rest = bhi[g, :, cols], blo[g, :, cols]
                dot = lambda x, y: jnp.dot(x, y, preferred_element_type=F32)
                out.append(dot(high, b_high) + (dot(high, b_rest) + dot(rest, b_high)))
        return out

    def renorm_normal(src, g, first=False):
        for j in range(2):
            real = src[0, j].reshape(128, 128)
            imag = src[1, j].reshape(128, 128)
            res = product(real, imag, g)
            for r in range(2):
                for a in range(4):
                    value = res[2 * r + a // 2][:, 128 * (a % 2) : 128 * (a % 2) + 128]
                    if first:
                        on_ref[r, j, a] = value
                    else:
                        on_ref[r, j, a] += value

    def renorm_comp(real, imag, g):
        res = product(real.reshape(128, 128), imag.reshape(128, 128), g)
        for r in range(2):
            for a in range(4):
                oc_ref[r, 0, a] += res[2 * r + a // 2][:, 128 * (a % 2) : 128 * (a % 2) + 128]

    renorm_normal(nall.at[s], s, first=True)
    copies[2].wait()

    for a in range(4):
        real = jnp.zeros((128, 128), F32)
        imag = jnp.zeros((128, 128), F32)
        for b in range(4):
            t_re, t_im = t_ref[0, 0, a, b], t_ref[1, 0, a, b]
            b_re, b_im = bas[0, b, pl.ds(0, 128)], bas[1, b, pl.ds(0, 128)]
            real += t_re * b_re - t_im * b_im
            imag += t_re * b_im + t_im * b_re
        oc_ref[0, 0, a] = real
        oc_ref[1, 0, a] = imag

    def swap(inv):
        wait_for(rows.at[inv, :, pl.ds(0, 15), 0], f_r.at[inv])
        remote(rows.at[inv, :, :, core], rows.at[inv, :, :, core], c_s.at[inv], c_r.at[inv], mate).start()

    def complementary(inv):
        wait_for(rows.at[inv, :, :, 1 - core], c_r.at[inv])
        flat = rows.at[inv].reshape(1024, 128)
        table = coef.reshape(256, 128)
        lines = [table[pl.ds(i, 32, stride=8), :] for i in range(4)]
        left = jnp.concatenate(
            [jnp.where(half == 0, lines[0], lines[2]), jnp.where(half == 0, lines[1], lines[3])], axis=0
        )
        out = part.at[inv].reshape(512, 128)
        for i in range(8):
            res = jnp.dot(left, flat[pl.ds(i, 128, stride=8), :], preferred_element_type=F32, precision=lax.Precision.HIGHEST)
            out[pl.ds(i, 64, stride=8), :] = res

    def back(inv, gi):
        @pl.loop(1, 16)
        def _(d):
            q = (chip + d) % 16
            remote(part.at[inv, :, :, q], done.at[gi, :, :, chip], k_s.at[inv], k_r.at[inv], on_chip(q)).start()

        done[gi, :, :, chip] = part[inv, :, :, chip]

    def wait_back(inv, gi):
        wait_for(done.at[gi, :, :, pl.ds(0, 15)], k_r.at[inv])

    def done_piece(gi, c, whose):
        return done.at[gi, c // 2, whose, pl.ds(8 * (c % 2), 8)]

    def x_piece(g, c):
        return xchain.at[g, c // 2, pl.ds(8 * (c % 2), 8)]

    def o_piece(gi, c):
        return ochain.at[gi, c // 2, pl.ds(8 * (c % 2), 8)]

    def mirrored(v, g):
        return g if v < 2 else 3 - g

    def originate(v, t):
        gi = (v + t) % 2
        g = 2 * (v // 2) + gi
        for c in range(4):
            if v in (0, 3):
                to = z_to[LEFT if v == 0 else RIGHT]
                remote(done_piece(gi, c, 1 - half), x_piece(g, c), xo_s.at[gi, c], x_r.at[g, c], to).start()
            else:
                if t == 0:
                    remote(done_piece(gi, c, 1 - half), x_piece(g, c), xo_s.at[gi, c], x_r.at[g, c], edge_beyond).start()
                to = z_to[RIGHT if v == 1 else LEFT]
                remote(done_piece(gi, c, half), o_piece(gi, c), oo_s.at[gi, c], o_r.at[gi, c], to).start()

    def x_take(v, g, on):
        g = mirrored(v, g)
        for c in range(4):
            wait_for(x_piece(g, c), x_r.at[g, c])
            if on is not None:
                to = z_to[RIGHT if (on == "inward") == (v < 2) else LEFT]
                remote(x_piece(g, c), x_piece(g, c), xf_s.at[g, c], x_r.at[g, c], to).start()

    def o_take(v, g):
        gi = mirrored(v, g) % 2
        for c in range(4):
            wait_for(o_piece(gi, c), o_r.at[gi, c])
            if v in (1, 2):
                to = z_to[LEFT if v == 1 else RIGHT]
                remote(o_piece(gi, c), o_piece(gi, c), of_s.at[gi, c], o_r.at[gi, c], to).start()

    def each(step):
        for v in range(4):
            @pl.when(s == v)
            def _(v=v):
                step(v, v in (0, 3))

    def early(v, at_edge):
        if at_edge:
            x_take(v, 3, "inward")
            o_take(v, 2)
        else:
            o_take(v, 2)
            x_take(v, 3, "inward")

    def late_first(v, at_edge):
        if at_edge:
            x_take(v, 1, "inward")
            x_take(v, 2, "inward")
        else:
            x_take(v, 0, "outward")
            o_take(v, 3)

    def late_second(v, at_edge):
        x_take(v, 0 if at_edge else 1, None)

    def late_third(v, at_edge):
        if at_edge:
            o_take(v, 3)
        else:
            x_take(v, 2, None)

    def from_end(g):
        return jnp.where(s < 2, g, 3 - g)

    def comp_own(g):
        g = from_end(g)
        gi = g % 2
        renorm_comp(done[gi, 0, half] + xchain[g, 0], done[gi, 1, half] + xchain[g, 1], g)

    def comp_other(g):
        g = from_end(g)
        gi = g % 2
        renorm_comp(ochain[gi, 0] + xchain[g, 0], ochain[gi, 1] + xchain[g, 1], g)

    def n_step(k, pieces):
        for c in pieces:
            for way in (RIGHT, LEFT):
                n_wait(way, k, c)
                if k < 2:
                    n_send(way, k + 1, c)

    def n_renorm(k):
        for way in (RIGHT, LEFT):
            @pl.when(n_can_recv(way, k))
            def _():
                slot = n_slot(way, k + 1)
                renorm_normal(nall.at[slot], slot)

    other = s + 1 - 2 * odd
    n_step(0, (0, 1))
    forward(1, other, 0)
    swap(0)
    n_step(0, (2, 3))
    forward(1, other, 1)
    wait_for(coef.at[:, pl.ds(0, 15)], ip_r)
    complementary(0)
    back(0, odd)
    n_renorm(0)
    swap(1)
    n_step(1, range(4))
    wait_back(0, odd)
    each(lambda v, at_edge: originate(v, 0))
    complementary(1)
    back(1, 1 - odd)
    n_renorm(1)
    each(early)
    wait_back(1, 1 - odd)
    each(lambda v, at_edge: originate(v, 1))
    each(late_first)
    n_step(2, range(4))
    n_renorm(2)
    comp_own(jnp.where(edge, 1, 0))
    comp_other(jnp.where(edge, 2, 3))
    each(late_second)
    comp_own(jnp.where(edge, 0, 1))
    each(late_third)
    comp_other(jnp.where(edge, 3, 2))

    for c in range(4):
        for way in (RIGHT, LEFT):
            for k in range(3):
                @pl.when(n_can_send(way, k))
                def _():
                    wait_for(n_piece(0, c), n_s.at[way, k, c])

    def sent(v, at_edge):
        for c in range(4):
            for gi in range(2):
                if at_edge or gi == v % 2:
                    wait_for(x_piece(0, c), xo_s.at[gi, c])
                if not at_edge:
                    wait_for(o_piece(0, c), oo_s.at[gi, c])
                    wait_for(o_piece(0, c), of_s.at[gi, c])
            for g in (1, 2, 3) if at_edge else (0, 3):
                wait_for(x_piece(0, c), xf_s.at[mirrored(v, g), c])

    each(sent)

    for inv in range(2):
        wait_for(rows.at[inv, :, pl.ds(0, 15), 0], f_s.at[inv])
        wait_for(rows.at[inv, :, :, core], c_s.at[inv])
        wait_for(part.at[inv, :, :, pl.ds(0, 15)], k_s.at[inv])
    wait_for(coef.at[:, pl.ds(0, 15)], ip_s)

    @pl.when((s == 0) | (s == 3))
    def _():
        wait_for(coef.at[:, 0], iz_s)


def on_device(normal_ops, integrals, site_terms, basis):
    inputs = (normal_ops.reshape(2, 2, 16, 8, 128), integrals, site_terms, basis)
    sem = pltpu.SemaphoreType.DMA
    vmem = pl.BlockSpec(memory_space=pltpu.VMEM)
    return pl.pallas_call(
        kernel,
        name="renormalize",
        out_shape=(
            jax.ShapeDtypeStruct((2, 2, 4, 128, 128), F32),
            jax.ShapeDtypeStruct((2, 1, 4, 128, 128), F32),
        ),
        in_specs=[pl.BlockSpec(memory_space=pltpu.HBM)] * 4,
        out_specs=(vmem, vmem),
        scratch_shapes=[
            pltpu.VMEM((2, 1, 128), F32),
            pltpu.SMEM((2, 1, 4, 4), F32),
            pltpu.VMEM((2, 4, 512, 128), F32),
            pltpu.VMEM((4, 256, 512), BF16),
            pltpu.VMEM((4, 256, 512), BF16),
            pltpu.VMEM((4, 2, 2, 16, 8, 128), F32),
            pltpu.VMEM((2, 2, 16, 2, 2, 8, 128), F32),
            pltpu.VMEM((2, 16, 8, 128), F32),
            pltpu.VMEM((2, 2, 2, 16, 8, 128), F32),
            pltpu.VMEM((2, 2, 2, 16, 8, 128), F32),
            pltpu.VMEM((2, 2, 16, 8, 128), F32),
            pltpu.VMEM((4, 2, 16, 8, 128), F32),
            sem((4,)),
            sem((2, 3, 4)), sem((2, 3, 4)),
            sem((2,)), sem((2,)),
            sem((2,)), sem((2,)),
            sem, sem, sem, sem,
            sem((2,)), sem((2,)),
            sem((2, 4)), sem((2, 4)), sem((2, 4)),
            sem((2, 4)), sem((4, 4)), sem((4, 4)),
        ],
        compiler_params=pltpu.CompilerParams(
            collective_id=0, has_side_effects=True, vmem_limit_bytes=32 * 2**20
        ),
    )(*(pltpu.with_memory_space_constraint(x, pltpu.HBM) for x in inputs))


def solution(mesh):
    placed = (
        P(None, "pair", None, "sec"),
        P(None, "pair", None),
        P(None, "pair", None, None),
        P(None, None, None, "sec"),
    )
    return jax.shard_map(
        on_device,
        mesh=mesh,
        in_specs=placed,
        out_specs=(P(None, "pair", None, None, "sec"), P(None, "pair", None, None, "sec")),
        check_vma=False,
    )
```

```python
import jax
import jax.numpy as jnp
from jax import lax
from jax.experimental import pallas as pl
from jax.experimental.pallas import tpu as pltpu
from jax.sharding import PartitionSpec as P

MESH = pl.DeviceIdType.MESH
F32 = jnp.float32
BF16 = jnp.bfloat16
RIGHT, LEFT = 0, 1
OFFSETS = sorted(
    ((y, x) for y in range(4) for x in range(4) if (y, x) != (0, 0)),
    key=lambda o: -(min(o[0], 4 - o[0]) + min(o[1], 4 - o[1])),
)


def split(x):
    high = x.astype(BF16)
    return high, (x - high.astype(F32)).astype(BF16)


def kernel(
    n_hbm, i_hbm, t_hbm, b_hbm, on_ref, oc_ref,
    i_ref, t_ref, bas, bcat, nall, rows, coef, part, done, ochain, xchain,
    in_sem, n_s, n_r, g_s, g_r, f_s, f_r, c_s, c_r, iz_s, iz_r, ip_s, ip_r, k_s, k_r, oo_s, op_s, op_r, of_s, o_r, xb_s, xo_s, xf_s, x_r, ready,
):
    p = lax.axis_index("pair")
    s = lax.axis_index("sec")
    half = p // 32
    chip = (p // 2) % 16
    core = p % 2
    pairing = s // 2
    odd = s % 2

    chips = [(chip // 4 + y) % 4 * 4 + (chip % 4 + x) % 4 for y, x in OFFSETS]

    other = s + 1 - 2 * odd
    skip = (s + 2) % 4
    inner_neighbour = (p, 3 - s)

    def on_chip(q):
        return (half * 32 + q * 2 + core, s)

    def on_pair(q):
        return (half * 32 + q * 2 + core, other)

    mate = (p - core + (1 - core), s)
    z_up = ((p + 32 * ((s + 1) // 4)) % 64, (s + 1) % 4)
    z_down = ((p + 32 * ((4 - s) // 4)) % 64, (s + 3) % 4)
    z_to = (z_up, z_down)
    edge = (s == 0) | (s == 3)
    beyond = ((p + 32) % 64, s + 1 - 2 * (s % 2))
    second = ((p + 32) % 64, (s + 2) % 4)

    def remote(src, dst, send, recv, to):
        return pltpu.make_async_remote_copy(
            src_ref=src, dst_ref=dst, send_sem=send, recv_sem=recv, device_id=to, device_id_type=MESH
        )

    def wait_for(ref, sem):
        pltpu.make_async_copy(ref, ref, sem).wait()

    copies = [
        pltpu.make_async_copy(src, dst, in_sem.at[k])
        for k, (src, dst) in enumerate(((i_hbm, i_ref), (n_hbm, nall.at[s]), (t_hbm, t_ref), (b_hbm, bas)))
    ]
    for copy in copies:
        copy.start()

    barrier = pltpu.get_barrier_semaphore()

    for to in [on_chip(q) for q in chips] + [beyond, second, (p, skip), z_up, z_down]:
        pl.semaphore_signal(barrier, inc=1, device_id=to, device_id_type=MESH)

    @pl.when(edge)
    def _():
        for q in chips:
            pl.semaphore_signal(barrier, inc=1, device_id=on_pair(q), device_id_type=MESH)

    @pl.when(core == 0)
    def _():
        pl.semaphore_signal(barrier, inc=1, device_id=mate, device_id_type=MESH)

    copies[0].wait()
    re = jnp.broadcast_to(i_ref[0], (8, 128))
    im = jnp.broadcast_to(i_ref[1], (8, 128))
    re_t, im_t = pltpu.roll(re, 64, 1), pltpu.roll(im, 64, 1)
    low = lax.broadcasted_iota(jnp.int32, (8, 128), 1) < 64
    row = lax.broadcasted_iota(jnp.int32, (8, 128), 0)
    tile = jnp.where(
        row == 0,
        jnp.where(low, re, -im_t),
        jnp.where(
            row == 1,
            jnp.where(low, im, re_t),
            jnp.where(row == 2, jnp.where(low, re_t, -im), jnp.where(low, im_t, re)),
        ),
    )
    coef[half, chip] = tile
    copies[1].wait()
    pl.semaphore_wait(barrier, jnp.where(edge, 20, 35) + core)

    @pl.when(core == 1)
    def _():
        pl.semaphore_signal(ready, inc=1, device_id=mate, device_id_type=MESH)


    @pl.when(edge)
    def _():
        remote(coef.at[half, chip], coef.at[half, chip], iz_s, iz_r, second).start()

    @pl.when(s == 3)
    def _():
        remote(coef.at[half, chip], coef.at[half, chip], iz_s, iz_r, z_up).start()

    @pl.when(s == 0)
    def _():
        remote(coef.at[half, chip], coef.at[half, chip], iz_s, iz_r, z_down).start()

    for q in chips:
        remote(nall.at[s, :, :, q], rows.at[0, :, chip, core], f_s.at[0], f_r.at[0], on_chip(q)).start()

    @pl.when(~edge)
    def _():
        for q in chips + [chip]:
            remote(nall.at[s, :, :, q], rows.at[1, :, chip, core], f_s.at[1], f_r.at[1], on_pair(q)).start()

    rows[0, :, chip, core] = nall[s, :, :, chip]

    def n_slot(way, k):
        return s - k if way == RIGHT else s + k

    def n_can_send(way, k):
        if k == 0:
            return s < 2 if way == RIGHT else s > 1
        return (s < 3) & (s >= k) if way == RIGHT else (s > 0) & (s + k <= 3)

    def n_can_recv(way, k):
        if k == 0:
            return ~edge
        return s - 1 >= k if way == RIGHT else s + 1 + k <= 3

    def n_send(way, k, c):
        @pl.when(n_can_send(way, k))
        def _():
            piece = nall.at[n_slot(way, k), c]
            remote(piece, piece, n_s.at[way, k, c], n_r.at[way, k, c], z_to[way]).start()

    def n_step(k):
        for c in range(2):
            for way in (RIGHT, LEFT):
                @pl.when(n_can_recv(way, k))
                def _():
                    wait_for(nall.at[n_slot(way, k + 1), c], n_r.at[way, k, c])

                if k < 2:
                    n_send(way, k + 1, c)

    for c in range(2):
        for way in (RIGHT, LEFT):
            n_send(way, 0, c)

    def give_back():
        for q in chips:
            remote(rows.at[1, :, q, core], nall.at[other, :, :, chip], g_s, g_r, on_chip(q)).start()
        nall[other, :, :, chip] = rows[1, :, chip, core]

    def n_pair():
        wait_for(nall.at[other, :, :, pl.ds(0, 15)], g_r)

    wait_for(coef.at[1 - half, chip], iz_r)
    for q in chips:
        remote(coef.at[:, chip], coef.at[:, chip], ip_s, ip_r, on_chip(q)).start()

    copies[3].wait()
    for g in range(4):
        for r in range(2):
            for a in range(4):
                high, rest = split(bas[r, a, pl.ds(128 * g, 128)])
                for k, value in enumerate((high, high, rest)):
                    bcat[g, pl.ds(256 * k + 128 * r, 128), pl.ds(128 * a, 128)] = value

    def product(real, imag, g):
        left = jnp.concatenate(
            [jnp.concatenate([real, -imag], axis=1), jnp.concatenate([imag, real], axis=1)], axis=0
        )
        high, rest = split(left)
        left = jnp.concatenate([high, rest, high], axis=1)
        return [
            jnp.dot(left, bcat[g, :, pl.ds(256 * pair, 256)], preferred_element_type=F32) for pair in range(2)
        ]

    def renorm_normal(src, g, first=False):
        res = product(src[0].reshape(256, 128), src[1].reshape(256, 128), g)
        for r in range(2):
            for j in range(2):
                for a in range(4):
                    value = res[a // 2][256 * r + 128 * j : 256 * r + 128 * j + 128, 128 * (a % 2) : 128 * (a % 2) + 128]
                    if first:
                        on_ref[r, j, a] = value
                    else:
                        on_ref[r, j, a] += value

    def renorm_comp(real, imag, g):
        res = product(real.reshape(128, 128), imag.reshape(128, 128), g)
        for r in range(2):
            for a in range(4):
                oc_ref[r, 0, a] += res[a // 2][128 * r : 128 * r + 128, 128 * (a % 2) : 128 * (a % 2) + 128]

    def site_part():
        copies[2].wait()
        for a in range(4):
            real = jnp.zeros((128, 128), F32)
            imag = jnp.zeros((128, 128), F32)
            for b in range(4):
                t_re, t_im = t_ref[0, 0, a, b], t_ref[1, 0, a, b]
                b_re, b_im = bas[0, b, pl.ds(0, 128)], bas[1, b, pl.ds(0, 128)]
                real += t_re * b_re - t_im * b_im
                imag += t_re * b_im + t_im * b_re
            oc_ref[0, 0, a] = real
            oc_ref[1, 0, a] = imag

    def swap(inv):
        remote(rows.at[inv, :, :, core], rows.at[inv, :, :, core], c_s.at[inv], c_r.at[inv], mate).start()

    def complementary(inv):
        wait_for(rows.at[inv, :, :, 1 - core], c_r.at[inv])
        flat = rows.at[inv].reshape(1024, 128)
        table = coef.reshape(256, 128)
        lines = [table[pl.ds(i, 32, stride=8), :] for i in range(4)]
        left = jnp.concatenate(
            [jnp.where(half == 0, lines[0], lines[2]), jnp.where(half == 0, lines[1], lines[3])], axis=0
        )
        out = part.at[inv].reshape(512, 128)
        for i in range(8):
            res = jnp.dot(left, flat[pl.ds(i, 128, stride=8), :], preferred_element_type=F32, precision=lax.Precision.HIGHEST)
            out[pl.ds(i, 64, stride=8), :] = res

    def back(inv, gi):
        for q in chips:
            remote(part.at[inv, :, :, q], done.at[gi, :, :, chip], k_s.at[inv], k_r.at[inv], on_chip(q)).start()
        done[gi, :, :, chip] = part[inv, :, :, chip]

    def wait_back(inv, gi):
        wait_for(done.at[gi, :, :, pl.ds(0, 15)], k_r.at[inv])

    def done_piece(gi, c, whose):
        return done.at[gi, c, whose]

    def x_piece(g, c):
        return xchain.at[g, c]

    def o_piece(gi, c):
        return ochain.at[gi, c]

    def mirrored(v, g):
        return g if v < 2 else 3 - g

    def originate(v, t):
        gi = (v + t) % 2
        g = 2 * (v // 2) + gi
        for c in range(2):
            theirs, ours = done_piece(gi, c, 1 - half), done_piece(gi, c, half)
            if v in (0, 3):
                away = z_to[LEFT if v == 0 else RIGHT]
                far = beyond if t == 0 else second
                remote(theirs, x_piece(g, c), xb_s.at[t, c], x_r.at[g, c], far).start()
                if t == 0:
                    remote(ours, o_piece(gi, c), oo_s.at[c], o_r.at[gi, c], (p, skip)).start()
                    remote(ours, ours, op_s.at[c], op_r.at[c], (p, other)).start()
                remote(theirs, x_piece(g, c), xo_s.at[t, c], x_r.at[g, c], away).start()
            elif t == 0:
                remote(theirs, x_piece(g, c), xb_s.at[t, c], x_r.at[g, c], beyond).start()
                remote(ours, o_piece(gi, c), oo_s.at[c], o_r.at[gi, c], inner_neighbour).start()

    def x_take(v, g, on):
        g = mirrored(v, g)
        for c in range(2):
            wait_for(x_piece(g, c), x_r.at[g, c])
            if on is not None:
                to = z_to[RIGHT if (on == "inward") == (v < 2) else LEFT]
                remote(x_piece(g, c), x_piece(g, c), xf_s.at[g, c], x_r.at[g, c], to).start()

    def o_take(v, g):
        gi = mirrored(v, g) % 2
        for c in range(2):
            wait_for(o_piece(gi, c), o_r.at[gi, c])
            if v in (1, 2):
                to = z_to[LEFT if v == 1 else RIGHT]
                remote(o_piece(gi, c), o_piece(gi, c), of_s.at[gi, c], o_r.at[gi, c], to).start()

    def each(step):
        for v in range(4):
            @pl.when(s == v)
            def _(v=v):
                step(v, v in (0, 3))

    def early(v, at_edge):
        if at_edge:
            x_take(v, 3, "inward")
            x_take(v, 1, "inward")
        else:
            o_take(v, 2)
            x_take(v, 0, "outward")
            o_take(v, 3)
            for c in range(2):
                wait_for(done_piece(0, c, half), op_r.at[c])

    def late_first(v, at_edge):
        if at_edge:
            x_take(v, 0, None)
        else:
            x_take(v, 3, None)
            x_take(v, 1, None)

    def late_second(v, at_edge):
        if at_edge:
            o_take(v, 3)

    def late_third(v, at_edge):
        if at_edge:
            o_take(v, 2)
        x_take(v, 2, None)

    def from_end(g):
        return jnp.where(s < 2, g, 3 - g)

    def comp_own(g):
        g = from_end(g)
        gi = g % 2
        renorm_comp(done[gi, 0, half] + xchain[g, 0], done[gi, 1, half] + xchain[g, 1], g)

    def comp_other(g):
        g = from_end(g)
        gi = g % 2
        renorm_comp(ochain[gi, 0] + xchain[g, 0], ochain[gi, 1] + xchain[g, 1], g)

    def n_renorm(k):
        for way in (RIGHT, LEFT):
            @pl.when(n_can_recv(way, k))
            def _():
                slot = n_slot(way, k + 1)
                renorm_normal(nall.at[slot], slot)

    @pl.when(core == 0)
    def _():
        pl.semaphore_wait(ready, 1)

    wait_for(rows.at[0, :, pl.ds(0, 15), 0], f_r.at[0])
    swap(0)
    n_step(0)
    wait_for(coef.at[:, pl.ds(0, 15)], ip_r)
    complementary(0)
    back(0, odd)

    @pl.when(edge)
    def _():
        wait_for(rows.at[1, :, :, 0], f_r.at[1])
        swap(1)
        give_back()
        complementary(1)
        back(1, 1 - odd)

    @pl.when(~edge)
    def _():
        renorm_normal(nall.at[s], s, first=True)
        n_renorm(0)

    wait_back(0, odd)
    each(lambda v, at_edge: originate(v, 0))
    n_step(1)
    site_part()

    @pl.when(edge)
    def _():
        renorm_normal(nall.at[s], s, first=True)
        n_pair()
        renorm_normal(nall.at[other], other)
        wait_back(1, 1 - odd)

    each(lambda v, at_edge: originate(v, 1))
    each(early)
    n_renorm(1)
    comp_own(jnp.where(edge, 1, 0))
    n_step(2)
    n_renorm(2)
    each(late_first)
    comp_own(jnp.where(edge, 0, 1))
    each(late_second)
    comp_other(3)
    each(late_third)
    comp_other(2)

    for c in range(2):
        for way in (RIGHT, LEFT):
            for k in range(3):
                @pl.when(n_can_send(way, k))
                def _():
                    wait_for(nall.at[0, c], n_s.at[way, k, c])

    def sent(v, at_edge):
        for c in range(2):
            wait_for(x_piece(0, c), xb_s.at[0, c])
            wait_for(o_piece(0, c), oo_s.at[c])
            if at_edge:
                wait_for(o_piece(0, c), op_s.at[c])
                wait_for(x_piece(0, c), xb_s.at[1, c])
                for t in range(2):
                    wait_for(x_piece(0, c), xo_s.at[t, c])
                for g in (1, 3):
                    wait_for(x_piece(0, c), xf_s.at[mirrored(v, g), c])
            else:
                for gi in range(2):
                    wait_for(o_piece(0, c), of_s.at[gi, c])
                wait_for(x_piece(0, c), xf_s.at[mirrored(v, 0), c])

    each(sent)

    def sent_exchange(inv):
        wait_for(rows.at[inv, :, :, core], c_s.at[inv])
        wait_for(part.at[inv, :, :, pl.ds(0, 15)], k_s.at[inv])

    wait_for(rows.at[0, :, pl.ds(0, 15), 0], f_s.at[0])
    sent_exchange(0)

    @pl.when(edge)
    def _():
        sent_exchange(1)
        wait_for(nall.at[other, :, :, pl.ds(0, 15)], g_s)

    @pl.when(~edge)
    def _():
        wait_for(rows.at[1, :, :, 0], f_s.at[1])

    wait_for(coef.at[:, pl.ds(0, 15)], ip_s)

    @pl.when((s == 0) | (s == 3))
    def _():
        wait_for(coef.at[:, 0], iz_s)


def on_device(normal_ops, integrals, site_terms, basis):
    inputs = (normal_ops.reshape(2, 2, 16, 8, 128), integrals, site_terms, basis)
    shapes = (
        jax.ShapeDtypeStruct((2, 2, 4, 128, 128), F32),
        jax.ShapeDtypeStruct((2, 1, 4, 128, 128), F32),
    )
    sem = pltpu.SemaphoreType.DMA
    vmem = pl.BlockSpec(memory_space=pltpu.VMEM)
    return pl.pallas_call(
        kernel,
        name="renormalize",
        out_shape=shapes,
        in_specs=[pl.BlockSpec(memory_space=pltpu.HBM)] * 4,
        out_specs=(vmem, vmem),
        scratch_shapes=[
            pltpu.VMEM((2, 1, 128), F32),
            pltpu.SMEM((2, 1, 4, 4), F32),
            pltpu.VMEM((2, 4, 512, 128), F32),
            pltpu.VMEM((4, 768, 512), BF16),
            pltpu.VMEM((4, 2, 2, 16, 8, 128), F32),
            pltpu.VMEM((2, 2, 16, 2, 2, 8, 128), F32),
            pltpu.VMEM((2, 16, 8, 128), F32),
            pltpu.VMEM((2, 2, 2, 16, 8, 128), F32),
            pltpu.VMEM((2, 2, 2, 16, 8, 128), F32),
            pltpu.VMEM((2, 2, 16, 8, 128), F32),
            pltpu.VMEM((4, 2, 16, 8, 128), F32),
            sem((4,)),
            sem((2, 3, 2)), sem((2, 3, 2)),
            sem, sem,
            sem((2,)), sem((2,)),
            sem((2,)), sem((2,)),
            sem, sem, sem, sem,
            sem((2,)), sem((2,)),
            sem((2,)), sem((2,)), sem((2,)), sem((2, 2)), sem((2, 2)),
            sem((2, 2)), sem((2, 2)), sem((4, 2)), sem((4, 2)),
            pltpu.SemaphoreType.REGULAR,
        ],
        compiler_params=pltpu.CompilerParams(
            collective_id=0, has_side_effects=True, vmem_limit_bytes=32 * 2**20
        ),
    )(*(pltpu.with_memory_space_constraint(x, pltpu.HBM) for x in inputs))


def solution(mesh):
    placed = (
        P(None, "pair", None, "sec"),
        P(None, "pair", None),
        P(None, "pair", None, None),
        P(None, None, None, "sec"),
    )
    return jax.shard_map(
        on_device,
        mesh=mesh,
        in_specs=placed,
        out_specs=(P(None, "pair", None, None, "sec"), P(None, "pair", None, None, "sec")),
        check_vma=False,
    )
```

```python
import jax
import jax.numpy as jnp
from jax import lax
from jax.experimental import pallas as pl
from jax.experimental.pallas import tpu as pltpu
from jax.sharding import PartitionSpec as P

MESH = pl.DeviceIdType.MESH
F32 = jnp.float32
BF16 = jnp.bfloat16
RIGHT, LEFT = 0, 1
OFFSETS = sorted(
    ((y, x) for y in range(4) for x in range(4) if (y, x) != (0, 0)),
    key=lambda o: -(min(o[0], 4 - o[0]) + min(o[1], 4 - o[1])),
)


def split(x):
    high = x.astype(BF16)
    return high, (x - high.astype(F32)).astype(BF16)


def kernel(
    n_hbm, i_hbm, t_hbm, b_hbm, on_ref, oc_ref,
    i_ref, t_ref, bas, bcat, nall, rows, coef, part, done, ochain, xchain,
    in_sem, n_s, n_r, g_s, g_r, f_s, f_r, c_s, c_r, iz_s, iz_r, ip_s, ip_r, k_s, k_r, oo_s, op_s, op_r, of_s, o_r, xb_s, xo_s, xf_s, xi_s, x_r, ready,
):
    p = lax.axis_index("pair")
    s = lax.axis_index("sec")
    half = p // 32
    chip = (p // 2) % 16
    core = p % 2
    pairing = s // 2
    odd = s % 2

    chips = [(chip // 4 + y) % 4 * 4 + (chip % 4 + x) % 4 for y, x in OFFSETS]

    other = s + 1 - 2 * odd
    skip = (s + 2) % 4
    inner_neighbour = (p, 3 - s)

    def on_chip(q):
        return (half * 32 + q * 2 + core, s)

    def on_pair(q):
        return (half * 32 + q * 2 + core, other)

    mate = (p - core + (1 - core), s)
    z_up = ((p + 32 * ((s + 1) // 4)) % 64, (s + 1) % 4)
    z_down = ((p + 32 * ((4 - s) // 4)) % 64, (s + 3) % 4)
    z_to = (z_up, z_down)
    edge = (s == 0) | (s == 3)
    beyond = ((p + 32) % 64, s + 1 - 2 * (s % 2))
    second = ((p + 32) % 64, (s + 2) % 4)

    def remote(src, dst, send, recv, to):
        return pltpu.make_async_remote_copy(
            src_ref=src, dst_ref=dst, send_sem=send, recv_sem=recv, device_id=to, device_id_type=MESH
        )

    def wait_for(ref, sem):
        pltpu.make_async_copy(ref, ref, sem).wait()

    copies = [
        pltpu.make_async_copy(src, dst, in_sem.at[k])
        for k, (src, dst) in enumerate(((i_hbm, i_ref), (n_hbm, nall.at[s]), (t_hbm, t_ref), (b_hbm, bas)))
    ]
    for copy in copies:
        copy.start()

    barrier = pltpu.get_barrier_semaphore()

    for to in [on_chip(q) for q in chips] + [beyond, second, (p, skip), z_up, z_down]:
        pl.semaphore_signal(barrier, inc=1, device_id=to, device_id_type=MESH)

    @pl.when(edge)
    def _():
        for q in chips:
            pl.semaphore_signal(barrier, inc=1, device_id=on_pair(q), device_id_type=MESH)

    @pl.when(core == 0)
    def _():
        pl.semaphore_signal(barrier, inc=1, device_id=mate, device_id_type=MESH)

    copies[0].wait()
    re = jnp.broadcast_to(i_ref[0], (8, 128))
    im = jnp.broadcast_to(i_ref[1], (8, 128))
    re_t, im_t = pltpu.roll(re, 64, 1), pltpu.roll(im, 64, 1)
    low = lax.broadcasted_iota(jnp.int32, (8, 128), 1) < 64
    row = lax.broadcasted_iota(jnp.int32, (8, 128), 0)
    tile = jnp.where(
        row == 0,
        jnp.where(low, re, -im_t),
        jnp.where(
            row == 1,
            jnp.where(low, im, re_t),
            jnp.where(row == 2, jnp.where(low, re_t, -im), jnp.where(low, im_t, re)),
        ),
    )
    coef[half, chip] = tile
    copies[1].wait()
    pl.semaphore_wait(barrier, jnp.where(edge, 20, 35) + core)

    @pl.when(core == 1)
    def _():
        pl.semaphore_signal(ready, inc=1, device_id=mate, device_id_type=MESH)


    @pl.when(edge)
    def _():
        remote(coef.at[half, chip], coef.at[half, chip], iz_s, iz_r, second).start()

    @pl.when(s == 3)
    def _():
        remote(coef.at[half, chip], coef.at[half, chip], iz_s, iz_r, z_up).start()

    @pl.when(s == 0)
    def _():
        remote(coef.at[half, chip], coef.at[half, chip], iz_s, iz_r, z_down).start()

    for q in chips:
        remote(nall.at[s, :, :, q], rows.at[0, :, chip, core], f_s.at[0], f_r.at[0], on_chip(q)).start()

    @pl.when(~edge)
    def _():
        for q in chips + [chip]:
            remote(nall.at[s, :, :, q], rows.at[1, :, chip, core], f_s.at[1], f_r.at[1], on_pair(q)).start()

    rows[0, :, chip, core] = nall[s, :, :, chip]

    def n_slot(way, k):
        return s - k if way == RIGHT else s + k

    def n_can_send(way, k):
        if k == 0:
            return s < 2 if way == RIGHT else s > 1
        return (s < 3) & (s >= k) if way == RIGHT else (s > 0) & (s + k <= 3)

    def n_can_recv(way, k):
        if k == 0:
            return ~edge
        return s - 1 >= k if way == RIGHT else s + 1 + k <= 3

    def n_send(way, k, c):
        @pl.when(n_can_send(way, k))
        def _():
            piece = nall.at[n_slot(way, k), c]
            remote(piece, piece, n_s.at[way, k, c], n_r.at[way, k, c], z_to[way]).start()

    def n_step(k):
        for c in range(2):
            for way in (RIGHT, LEFT):
                @pl.when(n_can_recv(way, k))
                def _():
                    wait_for(nall.at[n_slot(way, k + 1), c], n_r.at[way, k, c])

                if k < 2:
                    n_send(way, k + 1, c)

    for c in range(2):
        for way in (RIGHT, LEFT):
            n_send(way, 0, c)

    def give_back():
        for q in chips:
            remote(rows.at[1, :, q, core], nall.at[other, :, :, chip], g_s, g_r, on_chip(q)).start()
        nall[other, :, :, chip] = rows[1, :, chip, core]

    def n_pair():
        wait_for(nall.at[other, :, :, pl.ds(0, 15)], g_r)

    wait_for(coef.at[1 - half, chip], iz_r)
    for q in chips:
        remote(coef.at[:, chip], coef.at[:, chip], ip_s, ip_r, on_chip(q)).start()

    copies[3].wait()
    for g in range(4):
        for r in range(2):
            for a in range(4):
                high, rest = split(bas[r, a, pl.ds(128 * g, 128)])
                for k, value in enumerate((high, high, rest)):
                    bcat[g, pl.ds(256 * k + 128 * r, 128), pl.ds(128 * a, 128)] = value

    def product(real, imag, g):
        left = jnp.concatenate(
            [jnp.concatenate([real, -imag], axis=1), jnp.concatenate([imag, real], axis=1)], axis=0
        )
        high, rest = split(left)
        left = jnp.concatenate([high, rest, high], axis=1)
        return [
            jnp.dot(left, bcat[g, :, pl.ds(256 * pair, 256)], preferred_element_type=F32) for pair in range(2)
        ]

    def renorm_normal(src, g, first=False):
        res = product(src[0].reshape(256, 128), src[1].reshape(256, 128), g)
        for r in range(2):
            for j in range(2):
                for a in range(4):
                    value = res[a // 2][256 * r + 128 * j : 256 * r + 128 * j + 128, 128 * (a % 2) : 128 * (a % 2) + 128]
                    if first:
                        on_ref[r, j, a] = value
                    else:
                        on_ref[r, j, a] += value

    def renorm_comp(real, imag, g):
        res = product(real.reshape(128, 128), imag.reshape(128, 128), g)
        for r in range(2):
            for a in range(4):
                oc_ref[r, 0, a] += res[a // 2][128 * r : 128 * r + 128, 128 * (a % 2) : 128 * (a % 2) + 128]

    def site_part():
        copies[2].wait()
        for a in range(4):
            real = jnp.zeros((128, 128), F32)
            imag = jnp.zeros((128, 128), F32)
            for b in range(4):
                t_re, t_im = t_ref[0, 0, a, b], t_ref[1, 0, a, b]
                b_re, b_im = bas[0, b, pl.ds(0, 128)], bas[1, b, pl.ds(0, 128)]
                real += t_re * b_re - t_im * b_im
                imag += t_re * b_im + t_im * b_re
            oc_ref[0, 0, a] = real
            oc_ref[1, 0, a] = imag

    def swap(inv):
        remote(rows.at[inv, :, :, core], rows.at[inv, :, :, core], c_s.at[inv], c_r.at[inv], mate).start()

    def complementary(inv):
        wait_for(rows.at[inv, :, :, 1 - core], c_r.at[inv])
        flat = rows.at[inv].reshape(1024, 128)
        table = coef.reshape(256, 128)
        lines = [table[pl.ds(i, 32, stride=8), :] for i in range(4)]
        left = jnp.concatenate(
            [jnp.where(half == 0, lines[0], lines[2]), jnp.where(half == 0, lines[1], lines[3])], axis=0
        )
        out = part.at[inv].reshape(512, 128)
        for i in range(8):
            res = jnp.dot(left, flat[pl.ds(i, 128, stride=8), :], preferred_element_type=F32, precision=lax.Precision.HIGHEST)
            out[pl.ds(i, 64, stride=8), :] = res

    def back(inv, gi):
        for q in chips:
            remote(part.at[inv, :, :, q], done.at[gi, :, :, chip], k_s.at[inv], k_r.at[inv], on_chip(q)).start()
        done[gi, :, :, chip] = part[inv, :, :, chip]

    def wait_back(inv, gi):
        wait_for(done.at[gi, :, :, pl.ds(0, 15)], k_r.at[inv])

    def done_piece(gi, c, whose):
        return done.at[gi, c, whose]

    def x_piece(g, c):
        return xchain.at[g, c]

    def o_piece(gi, c):
        return ochain.at[gi, c]

    def mirrored(v, g):
        return g if v < 2 else 3 - g

    def originate(v, t):
        gi = (v + t) % 2
        g = 2 * (v // 2) + gi
        for c in range(2):
            theirs, ours = done_piece(gi, c, 1 - half), done_piece(gi, c, half)
            if v in (0, 3):
                away = z_to[LEFT if v == 0 else RIGHT]
                if t == 0:
                    remote(theirs, x_piece(g, c), xb_s.at[t, c], x_r.at[g, c], beyond).start()
                    remote(ours, ours, op_s.at[c], op_r.at[c], (p, other)).start()
                remote(theirs, x_piece(g, c), xo_s.at[t, c], x_r.at[g, c], away).start()
            elif t == 0:
                remote(theirs, x_piece(g, c), xb_s.at[t, c], x_r.at[g, c], beyond).start()
                remote(ours, o_piece(gi, c), oo_s.at[c], o_r.at[gi, c], inner_neighbour).start()

    def x_take(v, g, outward=(), inward=()):
        g = mirrored(v, g)
        for c in range(2):
            piece = x_piece(g, c)
            wait_for(piece, x_r.at[g, c])
            if c in outward:
                remote(piece, piece, xf_s.at[g, c], x_r.at[g, c], z_to[LEFT if v < 2 else RIGHT]).start()
            if c in inward:
                remote(piece, piece, xi_s.at[g, c], x_r.at[g, c], z_to[RIGHT if v < 2 else LEFT]).start()

    def o_take(v, g):
        gi = mirrored(v, g) % 2
        for c in range(2):
            wait_for(o_piece(gi, c), o_r.at[gi, c])
            if v in (1, 2):
                to = z_to[LEFT if v == 1 else RIGHT]
                remote(o_piece(gi, c), o_piece(gi, c), of_s.at[gi, c], o_r.at[gi, c], to).start()

    def edge_take(v):
        gi = mirrored(v, 0) % 2
        for c in range(2):
            piece = done_piece(gi, c, half)
            wait_for(piece, op_r.at[c])
            remote(piece, o_piece(gi, c), op_s.at[c], o_r.at[gi, c], inner_neighbour).start()

    def each(step):
        for v in range(4):
            @pl.when(s == v)
            def _(v=v):
                step(v, v in (0, 3))

    def early(v, at_edge):
        if at_edge:
            x_take(v, 1, inward=(0, 1))
            x_take(v, 3, inward=(0,))
        else:
            o_take(v, 2)
            edge_take(v)
            x_take(v, 0, outward=(0, 1), inward=(1,))
            o_take(v, 3)

    def late_first(v, at_edge):
        if at_edge:
            x_take(v, 2, inward=(0, 1))
            x_take(v, 0)
        else:
            x_take(v, 3)
            x_take(v, 1)

    def late_second(v, at_edge):
        if at_edge:
            o_take(v, 3)

    def late_third(v, at_edge):
        if at_edge:
            o_take(v, 2)
        else:
            x_take(v, 2)

    def from_end(g):
        return jnp.where(s < 2, g, 3 - g)

    def comp_own(g):
        g = from_end(g)
        gi = g % 2
        renorm_comp(done[gi, 0, half] + xchain[g, 0], done[gi, 1, half] + xchain[g, 1], g)

    def comp_other(g):
        g = from_end(g)
        gi = g % 2
        renorm_comp(ochain[gi, 0] + xchain[g, 0], ochain[gi, 1] + xchain[g, 1], g)

    def n_renorm(k):
        for way in (RIGHT, LEFT):
            @pl.when(n_can_recv(way, k))
            def _():
                slot = n_slot(way, k + 1)
                renorm_normal(nall.at[slot], slot)

    @pl.when(core == 0)
    def _():
        pl.semaphore_wait(ready, 1)

    wait_for(rows.at[0, :, pl.ds(0, 15), 0], f_r.at[0])
    swap(0)
    n_step(0)
    wait_for(coef.at[:, pl.ds(0, 15)], ip_r)
    complementary(0)
    back(0, odd)

    @pl.when(edge)
    def _():
        wait_for(rows.at[1, :, :, 0], f_r.at[1])
        swap(1)
        give_back()
        complementary(1)
        back(1, 1 - odd)

    @pl.when(~edge)
    def _():
        renorm_normal(nall.at[s], s, first=True)
        n_renorm(0)

    wait_back(0, odd)
    each(lambda v, at_edge: originate(v, 0))
    n_step(1)
    site_part()

    @pl.when(edge)
    def _():
        renorm_normal(nall.at[s], s, first=True)
        n_pair()
        renorm_normal(nall.at[other], other)
        wait_back(1, 1 - odd)

    each(lambda v, at_edge: originate(v, 1))
    each(early)
    n_renorm(1)
    comp_own(jnp.where(edge, 1, 0))
    n_step(2)
    n_renorm(2)
    each(late_first)
    comp_own(jnp.where(edge, 0, 1))
    each(late_second)
    comp_other(3)
    each(late_third)
    comp_other(2)

    for c in range(2):
        for way in (RIGHT, LEFT):
            for k in range(3):
                @pl.when(n_can_send(way, k))
                def _():
                    wait_for(nall.at[0, c], n_s.at[way, k, c])

    def sent(v, at_edge):
        for c in range(2):
            wait_for(x_piece(0, c), xb_s.at[0, c])
            wait_for(o_piece(0, c), op_s.at[c])
            if at_edge:
                for t in range(2):
                    wait_for(x_piece(0, c), xo_s.at[t, c])
                for g in (1, 2, 3) if c == 0 else (1, 2):
                    wait_for(x_piece(0, c), xi_s.at[mirrored(v, g), c])
            else:
                wait_for(o_piece(0, c), oo_s.at[c])
                for gi in range(2):
                    wait_for(o_piece(0, c), of_s.at[gi, c])
                wait_for(x_piece(0, c), xf_s.at[mirrored(v, 0), c])
                if c == 1:
                    wait_for(x_piece(0, c), xi_s.at[mirrored(v, 0), c])

    each(sent)

    def sent_exchange(inv):
        wait_for(rows.at[inv, :, :, core], c_s.at[inv])
        wait_for(part.at[inv, :, :, pl.ds(0, 15)], k_s.at[inv])

    wait_for(rows.at[0, :, pl.ds(0, 15), 0], f_s.at[0])
    sent_exchange(0)

    @pl.when(edge)
    def _():
        sent_exchange(1)
        wait_for(nall.at[other, :, :, pl.ds(0, 15)], g_s)

    @pl.when(~edge)
    def _():
        wait_for(rows.at[1, :, :, 0], f_s.at[1])

    wait_for(coef.at[:, pl.ds(0, 15)], ip_s)

    @pl.when((s == 0) | (s == 3))
    def _():
        wait_for(coef.at[:, 0], iz_s)


def on_device(normal_ops, integrals, site_terms, basis):
    inputs = (normal_ops.reshape(2, 2, 16, 8, 128), integrals, site_terms, basis)
    shapes = (
        jax.ShapeDtypeStruct((2, 2, 4, 128, 128), F32),
        jax.ShapeDtypeStruct((2, 1, 4, 128, 128), F32),
    )
    sem = pltpu.SemaphoreType.DMA
    vmem = pl.BlockSpec(memory_space=pltpu.VMEM)
    return pl.pallas_call(
        kernel,
        name="renormalize",
        out_shape=shapes,
        in_specs=[pl.BlockSpec(memory_space=pltpu.HBM)] * 4,
        out_specs=(vmem, vmem),
        scratch_shapes=[
            pltpu.VMEM((2, 1, 128), F32),
            pltpu.SMEM((2, 1, 4, 4), F32),
            pltpu.VMEM((2, 4, 512, 128), F32),
            pltpu.VMEM((4, 768, 512), BF16),
            pltpu.VMEM((4, 2, 2, 16, 8, 128), F32),
            pltpu.VMEM((2, 2, 16, 2, 2, 8, 128), F32),
            pltpu.VMEM((2, 16, 8, 128), F32),
            pltpu.VMEM((2, 2, 2, 16, 8, 128), F32),
            pltpu.VMEM((2, 2, 2, 16, 8, 128), F32),
            pltpu.VMEM((2, 2, 16, 8, 128), F32),
            pltpu.VMEM((4, 2, 16, 8, 128), F32),
            sem((4,)),
            sem((2, 3, 2)), sem((2, 3, 2)),
            sem, sem,
            sem((2,)), sem((2,)),
            sem((2,)), sem((2,)),
            sem, sem, sem, sem,
            sem((2,)), sem((2,)),
            sem((2,)), sem((2,)), sem((2,)), sem((2, 2)), sem((2, 2)),
            sem((2, 2)), sem((2, 2)), sem((4, 2)), sem((4, 2)), sem((4, 2)),
            pltpu.SemaphoreType.REGULAR,
        ],
        compiler_params=pltpu.CompilerParams(
            collective_id=0, has_side_effects=True, vmem_limit_bytes=32 * 2**20
        ),
    )(*(pltpu.with_memory_space_constraint(x, pltpu.HBM) for x in inputs))


def solution(mesh):
    placed = (
        P(None, "pair", None, "sec"),
        P(None, "pair", None),
        P(None, "pair", None, None),
        P(None, None, None, "sec"),
    )
    return jax.shard_map(
        on_device,
        mesh=mesh,
        in_specs=placed,
        out_specs=(P(None, "pair", None, None, "sec"), P(None, "pair", None, None, "sec")),
        check_vma=False,
    )
```

```python
import jax
import jax.numpy as jnp
from jax import lax
from jax.experimental import pallas as pl
from jax.experimental.pallas import tpu as pltpu
from jax.sharding import PartitionSpec as P

MESH = pl.DeviceIdType.MESH
F32 = jnp.float32
BF16 = jnp.bfloat16
RIGHT, LEFT = 0, 1
OFFSETS = sorted(
    ((y, x) for y in range(4) for x in range(4) if (y, x) != (0, 0)),
    key=lambda o: -(min(o[0], 4 - o[0]) + min(o[1], 4 - o[1])),
)


def split(x):
    high = x.astype(BF16)
    return high, (x - high.astype(F32)).astype(BF16)


def kernel(
    n_hbm, i_hbm, t_hbm, b_hbm, on_ref, oc_ref,
    i_ref, t_ref, bas, bcat, nall, rows, coef, part, done, ochain, xchain,
    in_sem, n_s, n_r, g_s, g_r, f_s, f_r, c_s, c_r, iz_s, iz_r, ip_s, ip_r, k_s, k_r, oo_s, op_s, op_r, of_s, o_r, xb_s, xo_s, xf_s, xi_s, x_r, ready,
):
    p = lax.axis_index("pair")
    s = lax.axis_index("sec")
    half = p // 32
    chip = (p // 2) % 16
    core = p % 2
    pairing = s // 2
    odd = s % 2

    chips = [(chip // 4 + y) % 4 * 4 + (chip % 4 + x) % 4 for y, x in OFFSETS]

    other = s + 1 - 2 * odd
    inner_neighbour = (p, 3 - s)

    def on_chip(q):
        return (half * 32 + q * 2 + core, s)

    def on_pair(q):
        return (half * 32 + q * 2 + core, other)

    mate = (p - core + (1 - core), s)
    z_up = ((p + 32 * ((s + 1) // 4)) % 64, (s + 1) % 4)
    z_down = ((p + 32 * ((4 - s) // 4)) % 64, (s + 3) % 4)
    z_to = (z_up, z_down)
    edge = (s == 0) | (s == 3)
    beyond = ((p + 32) % 64, s + 1 - 2 * (s % 2))
    second = ((p + 32) % 64, (s + 2) % 4)

    def remote(src, dst, send, recv, to):
        return pltpu.make_async_remote_copy(
            src_ref=src, dst_ref=dst, send_sem=send, recv_sem=recv, device_id=to, device_id_type=MESH
        )

    def wait_for(ref, sem):
        pltpu.make_async_copy(ref, ref, sem).wait()

    copies = [
        pltpu.make_async_copy(src, dst, in_sem.at[k])
        for k, (src, dst) in enumerate(((i_hbm, i_ref), (n_hbm, nall.at[s]), (t_hbm, t_ref), (b_hbm, bas)))
    ]
    for copy in copies:
        copy.start()

    barrier = pltpu.get_barrier_semaphore()

    for to in [on_chip(q) for q in chips] + [beyond, second, z_up, z_down]:
        pl.semaphore_signal(barrier, inc=1, device_id=to, device_id_type=MESH)

    @pl.when(edge)
    def _():
        for q in chips:
            pl.semaphore_signal(barrier, inc=1, device_id=on_pair(q), device_id_type=MESH)

    @pl.when(core == 0)
    def _():
        pl.semaphore_signal(barrier, inc=1, device_id=mate, device_id_type=MESH)

    copies[0].wait()
    re = jnp.broadcast_to(i_ref[0], (8, 128))
    im = jnp.broadcast_to(i_ref[1], (8, 128))
    re_t, im_t = pltpu.roll(re, 64, 1), pltpu.roll(im, 64, 1)
    low = lax.broadcasted_iota(jnp.int32, (8, 128), 1) < 64
    row = lax.broadcasted_iota(jnp.int32, (8, 128), 0)
    tile = jnp.where(
        row == 0,
        jnp.where(low, re, -im_t),
        jnp.where(
            row == 1,
            jnp.where(low, im, re_t),
            jnp.where(row == 2, jnp.where(low, re_t, -im), jnp.where(low, im_t, re)),
        ),
    )
    coef[half, chip] = tile
    copies[1].wait()
    pl.semaphore_wait(barrier, jnp.where(edge, 19, 34) + core)

    @pl.when(core == 1)
    def _():
        pl.semaphore_signal(ready, inc=1, device_id=mate, device_id_type=MESH)


    @pl.when(edge)
    def _():
        remote(coef.at[half, chip], coef.at[half, chip], iz_s, iz_r, second).start()

    @pl.when(s == 3)
    def _():
        remote(coef.at[half, chip], coef.at[half, chip], iz_s, iz_r, z_up).start()

    @pl.when(s == 0)
    def _():
        remote(coef.at[half, chip], coef.at[half, chip], iz_s, iz_r, z_down).start()

    for q in chips:
        remote(nall.at[s, :, :, q], rows.at[0, :, chip, core], f_s.at[0], f_r.at[0], on_chip(q)).start()

    @pl.when(~edge)
    def _():
        for q in chips + [chip]:
            remote(nall.at[s, :, :, q], rows.at[1, :, chip, core], f_s.at[1], f_r.at[1], on_pair(q)).start()

    rows[0, :, chip, core] = nall[s, :, :, chip]

    def n_slot(way, k):
        return s - k if way == RIGHT else s + k

    def n_can_send(way, k):
        if k == 0:
            return s < 2 if way == RIGHT else s > 1
        return (s < 3) & (s >= k) if way == RIGHT else (s > 0) & (s + k <= 3)

    def n_can_recv(way, k):
        if k == 0:
            return ~edge
        return s - 1 >= k if way == RIGHT else s + 1 + k <= 3

    def n_send(way, k, c):
        @pl.when(n_can_send(way, k))
        def _():
            piece = nall.at[n_slot(way, k), c]
            remote(piece, piece, n_s.at[way, k, c], n_r.at[way, k, c], z_to[way]).start()

    def n_step(k):
        for c in range(2):
            for way in (RIGHT, LEFT):
                @pl.when(n_can_recv(way, k))
                def _():
                    wait_for(nall.at[n_slot(way, k + 1), c], n_r.at[way, k, c])

                if k < 2:
                    n_send(way, k + 1, c)

    for c in range(2):
        for way in (RIGHT, LEFT):
            n_send(way, 0, c)

    def give_back():
        for q in chips:
            remote(rows.at[1, :, q, core], nall.at[other, :, :, chip], g_s, g_r, on_chip(q)).start()
        nall[other, :, :, chip] = rows[1, :, chip, core]

    def n_pair():
        wait_for(nall.at[other, :, :, pl.ds(0, 15)], g_r)

    wait_for(coef.at[1 - half, chip], iz_r)
    for q in chips:
        remote(coef.at[:, chip], coef.at[:, chip], ip_s, ip_r, on_chip(q)).start()

    copies[3].wait()
    for g in range(4):
        for r in range(2):
            for a in range(4):
                high, rest = split(bas[r, a, pl.ds(128 * g, 128)])
                for k, value in enumerate((high, high, rest)):
                    bcat[g, pl.ds(256 * k + 128 * r, 128), pl.ds(128 * a, 128)] = value

    def product(real, imag, g):
        left = jnp.concatenate(
            [jnp.concatenate([real, -imag], axis=1), jnp.concatenate([imag, real], axis=1)], axis=0
        )
        high, rest = split(left)
        left = jnp.concatenate([high, rest, high], axis=1)
        return [
            jnp.dot(left, bcat[g, :, pl.ds(256 * pair, 256)], preferred_element_type=F32) for pair in range(2)
        ]

    def renorm_normal(src, g, first=False):
        res = product(src[0].reshape(256, 128), src[1].reshape(256, 128), g)
        for r in range(2):
            for j in range(2):
                for a in range(4):
                    value = res[a // 2][256 * r + 128 * j : 256 * r + 128 * j + 128, 128 * (a % 2) : 128 * (a % 2) + 128]
                    if first:
                        on_ref[r, j, a] = value
                    else:
                        on_ref[r, j, a] += value

    def renorm_comp(real, imag, g):
        res = product(real.reshape(128, 128), imag.reshape(128, 128), g)
        for r in range(2):
            for a in range(4):
                oc_ref[r, 0, a] += res[a // 2][128 * r : 128 * r + 128, 128 * (a % 2) : 128 * (a % 2) + 128]

    def site_part():
        copies[2].wait()
        for a in range(4):
            real = jnp.zeros((128, 128), F32)
            imag = jnp.zeros((128, 128), F32)
            for b in range(4):
                t_re, t_im = t_ref[0, 0, a, b], t_ref[1, 0, a, b]
                b_re, b_im = bas[0, b, pl.ds(0, 128)], bas[1, b, pl.ds(0, 128)]
                real += t_re * b_re - t_im * b_im
                imag += t_re * b_im + t_im * b_re
            oc_ref[0, 0, a] = real
            oc_ref[1, 0, a] = imag

    def swap(inv):
        remote(rows.at[inv, :, :, core], rows.at[inv, :, :, core], c_s.at[inv], c_r.at[inv], mate).start()

    def complementary(inv):
        wait_for(rows.at[inv, :, :, 1 - core], c_r.at[inv])
        flat = rows.at[inv].reshape(1024, 128)
        table = coef.reshape(256, 128)
        lines = [table[pl.ds(i, 32, stride=8), :] for i in range(4)]
        left = jnp.concatenate(
            [jnp.where(half == 0, lines[0], lines[2]), jnp.where(half == 0, lines[1], lines[3])], axis=0
        )
        high, rest = split(left)
        left3 = jnp.concatenate([high, rest, high], axis=1)
        out = part.at[inv].reshape(512, 128)
        for i in range(8):
            x_high, x_rest = split(flat[pl.ds(i, 128, stride=8), :])
            right = jnp.concatenate([x_high, x_high, x_rest], axis=0)
            res = jnp.dot(left3, right, preferred_element_type=F32)
            out[pl.ds(i, 64, stride=8), :] = res

    def back(inv, gi):
        for q in chips:
            remote(part.at[inv, :, :, q], done.at[gi, :, :, chip], k_s.at[inv], k_r.at[inv], on_chip(q)).start()
        done[gi, :, :, chip] = part[inv, :, :, chip]

    def wait_back(inv, gi):
        wait_for(done.at[gi, :, :, pl.ds(0, 15)], k_r.at[inv])

    def done_piece(gi, c, whose):
        return done.at[gi, c, whose]

    def x_piece(g, c):
        return xchain.at[g, c]

    def o_piece(gi, c):
        return ochain.at[gi, c]

    def mirrored(v, g):
        return g if v < 2 else 3 - g

    def originate(v, t):
        gi = (v + t) % 2
        g = 2 * (v // 2) + gi
        for c in range(2):
            theirs, ours = done_piece(gi, c, 1 - half), done_piece(gi, c, half)
            if v in (0, 3):
                away = z_to[LEFT if v == 0 else RIGHT]
                if t == 0:
                    remote(theirs, x_piece(g, c), xb_s.at[t, c], x_r.at[g, c], beyond).start()
                    remote(ours, ours, op_s.at[c], op_r.at[c], (p, other)).start()
                remote(theirs, x_piece(g, c), xo_s.at[t, c], x_r.at[g, c], away).start()
            elif t == 0:
                remote(theirs, x_piece(g, c), xb_s.at[t, c], x_r.at[g, c], beyond).start()
                remote(ours, o_piece(gi, c), oo_s.at[c], o_r.at[gi, c], inner_neighbour).start()

    def x_take(v, g, outward=(), inward=()):
        g = mirrored(v, g)
        for c in range(2):
            piece = x_piece(g, c)
            wait_for(piece, x_r.at[g, c])
            if c in outward:
                remote(piece, piece, xf_s.at[g, c], x_r.at[g, c], z_to[LEFT if v < 2 else RIGHT]).start()
            if c in inward:
                remote(piece, piece, xi_s.at[g, c], x_r.at[g, c], z_to[RIGHT if v < 2 else LEFT]).start()

    def o_take(v, g):
        gi = mirrored(v, g) % 2
        for c in range(2):
            wait_for(o_piece(gi, c), o_r.at[gi, c])
            if v in (1, 2):
                to = z_to[LEFT if v == 1 else RIGHT]
                remote(o_piece(gi, c), o_piece(gi, c), of_s.at[gi, c], o_r.at[gi, c], to).start()

    def edge_take(v):
        gi = mirrored(v, 0) % 2
        for c in range(2):
            piece = done_piece(gi, c, half)
            wait_for(piece, op_r.at[c])
            remote(piece, o_piece(gi, c), op_s.at[c], o_r.at[gi, c], inner_neighbour).start()

    def each(step):
        for v in range(4):
            @pl.when(s == v)
            def _(v=v):
                step(v, v in (0, 3))

    def early(v, at_edge):
        if at_edge:
            x_take(v, 1, inward=(0, 1))
            x_take(v, 3, inward=(0,))
        else:
            o_take(v, 2)
            edge_take(v)
            x_take(v, 0, outward=(0, 1), inward=(1,))
            o_take(v, 3)

    def late_first(v, at_edge):
        if at_edge:
            x_take(v, 2, inward=(0, 1))
            x_take(v, 0)
        else:
            x_take(v, 3)
            x_take(v, 1)

    def late_second(v, at_edge):
        if at_edge:
            o_take(v, 3)

    def late_third(v, at_edge):
        if at_edge:
            o_take(v, 2)
        else:
            x_take(v, 2)

    def from_end(g):
        return jnp.where(s < 2, g, 3 - g)

    def comp_own(g):
        g = from_end(g)
        gi = g % 2
        renorm_comp(done[gi, 0, half] + xchain[g, 0], done[gi, 1, half] + xchain[g, 1], g)

    def comp_other(g):
        g = from_end(g)
        gi = g % 2
        renorm_comp(ochain[gi, 0] + xchain[g, 0], ochain[gi, 1] + xchain[g, 1], g)

    def n_renorm(k):
        for way in (RIGHT, LEFT):
            @pl.when(n_can_recv(way, k))
            def _():
                slot = n_slot(way, k + 1)
                renorm_normal(nall.at[slot], slot)

    @pl.when(core == 0)
    def _():
        pl.semaphore_wait(ready, 1)

    wait_for(rows.at[0, :, pl.ds(0, 15), 0], f_r.at[0])
    swap(0)
    n_step(0)
    wait_for(coef.at[:, pl.ds(0, 15)], ip_r)
    complementary(0)
    back(0, odd)

    @pl.when(edge)
    def _():
        wait_for(rows.at[1, :, :, 0], f_r.at[1])
        swap(1)
        give_back()
        complementary(1)
        back(1, 1 - odd)

    @pl.when(~edge)
    def _():
        renorm_normal(nall.at[s], s, first=True)
        n_renorm(0)

    wait_back(0, odd)
    each(lambda v, at_edge: originate(v, 0))
    n_step(1)
    site_part()

    @pl.when(edge)
    def _():
        renorm_normal(nall.at[s], s, first=True)
        n_pair()
        renorm_normal(nall.at[other], other)
        wait_back(1, 1 - odd)

    each(lambda v, at_edge: originate(v, 1))
    each(early)
    n_renorm(1)
    comp_own(jnp.where(edge, 1, 0))
    n_step(2)
    n_renorm(2)
    each(late_first)
    comp_own(jnp.where(edge, 0, 1))
    each(late_second)
    comp_other(3)
    each(late_third)
    comp_other(2)

    for c in range(2):
        for way in (RIGHT, LEFT):
            for k in range(3):
                @pl.when(n_can_send(way, k))
                def _():
                    wait_for(nall.at[0, c], n_s.at[way, k, c])

    def sent(v, at_edge):
        for c in range(2):
            wait_for(x_piece(0, c), xb_s.at[0, c])
            wait_for(o_piece(0, c), op_s.at[c])
            if at_edge:
                for t in range(2):
                    wait_for(x_piece(0, c), xo_s.at[t, c])
                for g in (1, 2, 3) if c == 0 else (1, 2):
                    wait_for(x_piece(0, c), xi_s.at[mirrored(v, g), c])
            else:
                wait_for(o_piece(0, c), oo_s.at[c])
                for gi in range(2):
                    wait_for(o_piece(0, c), of_s.at[gi, c])
                wait_for(x_piece(0, c), xf_s.at[mirrored(v, 0), c])
                if c == 1:
                    wait_for(x_piece(0, c), xi_s.at[mirrored(v, 0), c])

    each(sent)

    def sent_exchange(inv):
        wait_for(rows.at[inv, :, :, core], c_s.at[inv])
        wait_for(part.at[inv, :, :, pl.ds(0, 15)], k_s.at[inv])

    wait_for(rows.at[0, :, pl.ds(0, 15), 0], f_s.at[0])
    sent_exchange(0)

    @pl.when(edge)
    def _():
        sent_exchange(1)
        wait_for(nall.at[other, :, :, pl.ds(0, 15)], g_s)

    @pl.when(~edge)
    def _():
        wait_for(rows.at[1, :, :, 0], f_s.at[1])

    wait_for(coef.at[:, pl.ds(0, 15)], ip_s)

    @pl.when((s == 0) | (s == 3))
    def _():
        wait_for(coef.at[:, 0], iz_s)


def on_device(normal_ops, integrals, site_terms, basis):
    inputs = (normal_ops.reshape(2, 2, 16, 8, 128), integrals, site_terms, basis)
    shapes = (
        jax.ShapeDtypeStruct((2, 2, 4, 128, 128), F32),
        jax.ShapeDtypeStruct((2, 1, 4, 128, 128), F32),
    )
    sem = pltpu.SemaphoreType.DMA
    vmem = pl.BlockSpec(memory_space=pltpu.VMEM)
    return pl.pallas_call(
        kernel,
        name="renormalize",
        out_shape=shapes,
        in_specs=[pl.BlockSpec(memory_space=pltpu.HBM)] * 4,
        out_specs=(vmem, vmem),
        scratch_shapes=[
            pltpu.VMEM((2, 1, 128), F32),
            pltpu.SMEM((2, 1, 4, 4), F32),
            pltpu.VMEM((2, 4, 512, 128), F32),
            pltpu.VMEM((4, 768, 512), BF16),
            pltpu.VMEM((4, 2, 2, 16, 8, 128), F32),
            pltpu.VMEM((2, 2, 16, 2, 2, 8, 128), F32),
            pltpu.VMEM((2, 16, 8, 128), F32),
            pltpu.VMEM((2, 2, 2, 16, 8, 128), F32),
            pltpu.VMEM((2, 2, 2, 16, 8, 128), F32),
            pltpu.VMEM((2, 2, 16, 8, 128), F32),
            pltpu.VMEM((4, 2, 16, 8, 128), F32),
            sem((4,)),
            sem((2, 3, 2)), sem((2, 3, 2)),
            sem, sem,
            sem((2,)), sem((2,)),
            sem((2,)), sem((2,)),
            sem, sem, sem, sem,
            sem((2,)), sem((2,)),
            sem((2,)), sem((2,)), sem((2,)), sem((2, 2)), sem((2, 2)),
            sem((2, 2)), sem((2, 2)), sem((4, 2)), sem((4, 2)), sem((4, 2)),
            pltpu.SemaphoreType.REGULAR,
        ],
        compiler_params=pltpu.CompilerParams(
            collective_id=0, has_side_effects=True, vmem_limit_bytes=32 * 2**20
        ),
    )(*(pltpu.with_memory_space_constraint(x, pltpu.HBM) for x in inputs))


def solution(mesh):
    placed = (
        P(None, "pair", None, "sec"),
        P(None, "pair", None),
        P(None, "pair", None, None),
        P(None, None, None, "sec"),
    )
    return jax.shard_map(
        on_device,
        mesh=mesh,
        in_specs=placed,
        out_specs=(P(None, "pair", None, None, "sec"), P(None, "pair", None, None, "sec")),
        check_vma=False,
    )
```

```python
import jax
import jax.numpy as jnp
from jax import lax
from jax.experimental import pallas as pl
from jax.experimental.pallas import tpu as pltpu
from jax.sharding import PartitionSpec as P

MESH = pl.DeviceIdType.MESH
F32 = jnp.float32
BF16 = jnp.bfloat16
RIGHT, LEFT = 0, 1
OFFSETS = sorted(
    ((y, x) for y in range(4) for x in range(4) if (y, x) != (0, 0)),
    key=lambda o: -(min(o[0], 4 - o[0]) + min(o[1], 4 - o[1])),
)


def split(x):
    high = x.astype(BF16)
    return high, (x - high.astype(F32)).astype(BF16)


def kernel(
    n_hbm, i_hbm, t_hbm, b_hbm, on_ref, oc_ref,
    i_ref, t_ref, bas, bcat, nall, rows, coef, part, done, ochain, xchain,
    in_sem, n_s, n_r, g_s, g_r, f_s, f_r, c_s, c_r, iz_s, iz_r, ip_s, ip_r, k_s, k_r, oo_s, op_s, op_r, of_s, o_r, xb_s, xo_s, xf_s, xi_s, x_r, ready,
):
    p = lax.axis_index("pair")
    s = lax.axis_index("sec")
    half = p // 32
    chip = (p // 2) % 16
    core = p % 2
    pairing = s // 2
    odd = s % 2

    chips = [(chip // 4 + y) % 4 * 4 + (chip % 4 + x) % 4 for y, x in OFFSETS]

    other = s + 1 - 2 * odd
    inner_neighbour = (p, 3 - s)

    def on_chip(q):
        return (half * 32 + q * 2 + core, s)

    def on_pair(q):
        return (half * 32 + q * 2 + core, other)

    mate = (p - core + (1 - core), s)
    z_up = ((p + 32 * ((s + 1) // 4)) % 64, (s + 1) % 4)
    z_down = ((p + 32 * ((4 - s) // 4)) % 64, (s + 3) % 4)
    z_to = (z_up, z_down)
    edge = (s == 0) | (s == 3)
    beyond = ((p + 32) % 64, s + 1 - 2 * (s % 2))
    second = ((p + 32) % 64, (s + 2) % 4)

    def remote(src, dst, send, recv, to):
        return pltpu.make_async_remote_copy(
            src_ref=src, dst_ref=dst, send_sem=send, recv_sem=recv, device_id=to, device_id_type=MESH
        )

    def wait_for(ref, sem):
        pltpu.make_async_copy(ref, ref, sem).wait()

    copies = [
        pltpu.make_async_copy(src, dst, in_sem.at[k])
        for k, (src, dst) in enumerate(((i_hbm, i_ref), (n_hbm, nall.at[s]), (t_hbm, t_ref), (b_hbm, bas)))
    ]
    for copy in copies:
        copy.start()

    barrier = pltpu.get_barrier_semaphore()

    for to in [on_chip(q) for q in chips] + [beyond, second, z_up, z_down]:
        pl.semaphore_signal(barrier, inc=1, device_id=to, device_id_type=MESH)

    @pl.when(edge)
    def _():
        for q in chips:
            pl.semaphore_signal(barrier, inc=1, device_id=on_pair(q), device_id_type=MESH)

    @pl.when(core == 0)
    def _():
        pl.semaphore_signal(barrier, inc=1, device_id=mate, device_id_type=MESH)

    copies[0].wait()
    re = jnp.broadcast_to(i_ref[0], (8, 128))
    im = jnp.broadcast_to(i_ref[1], (8, 128))
    re_t, im_t = pltpu.roll(re, 64, 1), pltpu.roll(im, 64, 1)
    low = lax.broadcasted_iota(jnp.int32, (8, 128), 1) < 64
    row = lax.broadcasted_iota(jnp.int32, (8, 128), 0)
    tile = jnp.where(
        row == 0,
        jnp.where(low, re, -im_t),
        jnp.where(
            row == 1,
            jnp.where(low, im, re_t),
            jnp.where(row == 2, jnp.where(low, re_t, -im), jnp.where(low, im_t, re)),
        ),
    )
    coef[half, chip] = tile
    copies[1].wait()
    pl.semaphore_wait(barrier, jnp.where(edge, 19, 34) + core)

    @pl.when(core == 1)
    def _():
        pl.semaphore_signal(ready, inc=1, device_id=mate, device_id_type=MESH)


    @pl.when(edge)
    def _():
        remote(coef.at[half, chip], coef.at[half, chip], iz_s, iz_r, second).start()

    @pl.when(s == 3)
    def _():
        remote(coef.at[half, chip], coef.at[half, chip], iz_s, iz_r, z_up).start()

    @pl.when(s == 0)
    def _():
        remote(coef.at[half, chip], coef.at[half, chip], iz_s, iz_r, z_down).start()

    for q in chips:
        remote(nall.at[s, :, :, q], rows.at[0, :, chip, core], f_s.at[0], f_r.at[0], on_chip(q)).start()

    @pl.when(~edge)
    def _():
        for q in chips + [chip]:
            remote(nall.at[s, :, :, q], rows.at[1, :, chip, core], f_s.at[1], f_r.at[1], on_pair(q)).start()

    rows[0, :, chip, core] = nall[s, :, :, chip]

    def n_slot(way, k):
        return s - k if way == RIGHT else s + k

    def n_can_send(way, k):
        if k == 0:
            return s < 2 if way == RIGHT else s > 1
        return (s < 3) & (s >= k) if way == RIGHT else (s > 0) & (s + k <= 3)

    def n_can_recv(way, k):
        if k == 0:
            return ~edge
        return s - 1 >= k if way == RIGHT else s + 1 + k <= 3

    def n_send(way, k, c):
        @pl.when(n_can_send(way, k))
        def _():
            piece = nall.at[n_slot(way, k), c]
            remote(piece, piece, n_s.at[way, k, c], n_r.at[way, k, c], z_to[way]).start()

    def n_step(k):
        for c in range(2):
            for way in (RIGHT, LEFT):
                @pl.when(n_can_recv(way, k))
                def _():
                    wait_for(nall.at[n_slot(way, k + 1), c], n_r.at[way, k, c])

                if k < 2:
                    n_send(way, k + 1, c)

    for c in range(2):
        for way in (RIGHT, LEFT):
            n_send(way, 0, c)

    def give_back():
        for q in chips:
            remote(rows.at[1, :, q, core], nall.at[other, :, :, chip], g_s, g_r, on_chip(q)).start()
        nall[other, :, :, chip] = rows[1, :, chip, core]

    def n_pair():
        wait_for(nall.at[other, :, :, pl.ds(0, 15)], g_r)

    wait_for(coef.at[1 - half, chip], iz_r)
    for q in chips:
        remote(coef.at[:, chip], coef.at[:, chip], ip_s, ip_r, on_chip(q)).start()

    copies[3].wait()
    for g in range(4):
        for r in range(2):
            for a in range(4):
                high, rest = split(bas[r, a, pl.ds(128 * g, 128)])
                for k, value in enumerate((high, high, rest)):
                    bcat[g, pl.ds(256 * k + 128 * r, 128), pl.ds(128 * a, 128)] = value

    def product(real, imag, g):
        left = jnp.concatenate(
            [jnp.concatenate([real, -imag], axis=1), jnp.concatenate([imag, real], axis=1)], axis=0
        )
        high, rest = split(left)
        left = jnp.concatenate([high, rest, high], axis=1)
        return [
            jnp.dot(left, bcat[g, :, pl.ds(256 * pair, 256)], preferred_element_type=F32) for pair in range(2)
        ]

    def renorm_normal(src, g, first=False):
        res = product(src[0].reshape(256, 128), src[1].reshape(256, 128), g)
        for r in range(2):
            for j in range(2):
                for a in range(4):
                    value = res[a // 2][256 * r + 128 * j : 256 * r + 128 * j + 128, 128 * (a % 2) : 128 * (a % 2) + 128]
                    if first:
                        on_ref[r, j, a] = value
                    else:
                        on_ref[r, j, a] += value

    def renorm_comp(real, imag, g):
        res = product(real.reshape(128, 128), imag.reshape(128, 128), g)
        for r in range(2):
            for a in range(4):
                oc_ref[r, 0, a] += res[a // 2][128 * r : 128 * r + 128, 128 * (a % 2) : 128 * (a % 2) + 128]

    def site_part():
        copies[2].wait()
        for a in range(4):
            real = jnp.zeros((128, 128), F32)
            imag = jnp.zeros((128, 128), F32)
            for b in range(4):
                t_re, t_im = t_ref[0, 0, a, b], t_ref[1, 0, a, b]
                b_re, b_im = bas[0, b, pl.ds(0, 128)], bas[1, b, pl.ds(0, 128)]
                real += t_re * b_re - t_im * b_im
                imag += t_re * b_im + t_im * b_re
            oc_ref[0, 0, a] = real
            oc_ref[1, 0, a] = imag

    def swap(inv):
        remote(rows.at[inv, :, :, core], rows.at[inv, :, :, core], c_s.at[inv], c_r.at[inv], mate).start()

    def complementary(inv):
        wait_for(rows.at[inv, :, :, 1 - core], c_r.at[inv])
        flat = rows.at[inv].reshape(1024, 128)
        table = coef.reshape(256, 128)
        lines = [table[pl.ds(i, 32, stride=8), :] for i in range(4)]
        left = jnp.concatenate(
            [jnp.where(half == 0, lines[0], lines[2]), jnp.where(half == 0, lines[1], lines[3])], axis=0
        )
        high, rest = split(left)
        left3 = jnp.concatenate([high, rest, high], axis=1)
        out = part.at[inv].reshape(512, 128)
        for i in range(8):
            x_high, x_rest = split(flat[pl.ds(i, 128, stride=8), :])
            right = jnp.concatenate([x_high, x_high, x_rest], axis=0)
            res = jnp.dot(left3, right, preferred_element_type=F32)
            out[pl.ds(i, 64, stride=8), :] = res

    def back(inv, gi):
        for q in chips:
            remote(part.at[inv, :, :, q], done.at[gi, :, :, chip], k_s.at[inv], k_r.at[inv], on_chip(q)).start()
        done[gi, :, :, chip] = part[inv, :, :, chip]

    def wait_back(inv, gi):
        wait_for(done.at[gi, :, :, pl.ds(0, 15)], k_r.at[inv])

    def done_piece(gi, c, whose):
        return done.at[gi, c, whose]

    def x_piece(g, c):
        return xchain.at[g, c]

    def o_piece(gi, c):
        return ochain.at[gi, c]

    def mirrored(v, g):
        return g if v < 2 else 3 - g

    def originate(v, t):
        gi = (v + t) % 2
        g = 2 * (v // 2) + gi
        for c in range(2):
            theirs, ours = done_piece(gi, c, 1 - half), done_piece(gi, c, half)
            if v in (0, 3):
                away = z_to[LEFT if v == 0 else RIGHT]
                if t == 0:
                    remote(theirs, x_piece(g, c), xb_s.at[t, c], x_r.at[g, c], beyond).start()
                    remote(ours, ours, op_s.at[c], op_r.at[c], (p, other)).start()
                remote(theirs, x_piece(g, c), xo_s.at[t, c], x_r.at[g, c], away).start()
            elif t == 0:
                remote(theirs, x_piece(g, c), xb_s.at[t, c], x_r.at[g, c], beyond).start()
                remote(ours, o_piece(gi, c), oo_s.at[c], o_r.at[gi, c], inner_neighbour).start()

    def x_take(v, g, outward=(), inward=()):
        g = mirrored(v, g)
        for c in range(2):
            piece = x_piece(g, c)
            wait_for(piece, x_r.at[g, c])
            if c in outward:
                remote(piece, piece, xf_s.at[g, c], x_r.at[g, c], z_to[LEFT if v < 2 else RIGHT]).start()
            if c in inward:
                remote(piece, piece, xi_s.at[g, c], x_r.at[g, c], z_to[RIGHT if v < 2 else LEFT]).start()

    def o_take(v, g):
        gi = mirrored(v, g) % 2
        for c in range(2):
            wait_for(o_piece(gi, c), o_r.at[gi, c])
            if v in (1, 2):
                to = z_to[LEFT if v == 1 else RIGHT]
                remote(o_piece(gi, c), o_piece(gi, c), of_s.at[gi, c], o_r.at[gi, c], to).start()

    def edge_take(v):
        gi = mirrored(v, 0) % 2
        for c in range(2):
            piece = done_piece(gi, c, half)
            wait_for(piece, op_r.at[c])
            remote(piece, o_piece(gi, c), op_s.at[c], o_r.at[gi, c], inner_neighbour).start()

    def each(step):
        for v in range(4):
            @pl.when(s == v)
            def _(v=v):
                step(v, v in (0, 3))

    def early(v, at_edge):
        if at_edge:
            x_take(v, 1, inward=(0, 1))
            x_take(v, 3, inward=(0,))
        else:
            edge_take(v)
            o_take(v, 2)
            x_take(v, 0, outward=(0, 1), inward=(1,))
            o_take(v, 3)

    def late_first(v, at_edge):
        if at_edge:
            x_take(v, 2, inward=(0, 1))
            x_take(v, 0)
        else:
            x_take(v, 3)
            x_take(v, 1)

    def late_second(v, at_edge):
        if at_edge:
            o_take(v, 2)

    def late_third(v, at_edge):
        if at_edge:
            o_take(v, 3)
        else:
            x_take(v, 2)

    def from_end(g):
        return jnp.where(s < 2, g, 3 - g)

    def comp_own(g):
        g = from_end(g)
        gi = g % 2
        renorm_comp(done[gi, 0, half] + xchain[g, 0], done[gi, 1, half] + xchain[g, 1], g)

    def comp_other(g):
        g = from_end(g)
        gi = g % 2
        renorm_comp(ochain[gi, 0] + xchain[g, 0], ochain[gi, 1] + xchain[g, 1], g)

    def n_renorm(k):
        for way in (RIGHT, LEFT):
            @pl.when(n_can_recv(way, k))
            def _():
                slot = n_slot(way, k + 1)
                renorm_normal(nall.at[slot], slot)

    @pl.when(core == 0)
    def _():
        pl.semaphore_wait(ready, 1)

    wait_for(rows.at[0, :, pl.ds(0, 15), 0], f_r.at[0])
    swap(0)
    n_step(0)
    wait_for(coef.at[:, pl.ds(0, 15)], ip_r)
    complementary(0)
    back(0, odd)

    @pl.when(edge)
    def _():
        wait_for(rows.at[1, :, :, 0], f_r.at[1])
        swap(1)
        give_back()
        complementary(1)
        back(1, 1 - odd)

    @pl.when(~edge)
    def _():
        renorm_normal(nall.at[s], s, first=True)
        n_renorm(0)

    wait_back(0, odd)
    each(lambda v, at_edge: originate(v, 0))
    n_step(1)
    site_part()

    @pl.when(edge)
    def _():
        renorm_normal(nall.at[s], s, first=True)
        n_pair()
        renorm_normal(nall.at[other], other)
        wait_back(1, 1 - odd)

    each(lambda v, at_edge: originate(v, 1))
    each(early)
    n_renorm(1)
    comp_own(jnp.where(edge, 1, 0))
    n_step(2)
    n_renorm(2)
    each(late_first)
    comp_own(jnp.where(edge, 0, 1))
    each(late_second)
    comp_other(jnp.where(edge, 2, 3))
    each(late_third)
    comp_other(jnp.where(edge, 3, 2))

    for c in range(2):
        for way in (RIGHT, LEFT):
            for k in range(3):
                @pl.when(n_can_send(way, k))
                def _():
                    wait_for(nall.at[0, c], n_s.at[way, k, c])

    def sent(v, at_edge):
        for c in range(2):
            wait_for(x_piece(0, c), xb_s.at[0, c])
            wait_for(o_piece(0, c), op_s.at[c])
            if at_edge:
                for t in range(2):
                    wait_for(x_piece(0, c), xo_s.at[t, c])
                for g in (1, 2, 3) if c == 0 else (1, 2):
                    wait_for(x_piece(0, c), xi_s.at[mirrored(v, g), c])
            else:
                wait_for(o_piece(0, c), oo_s.at[c])
                for gi in range(2):
                    wait_for(o_piece(0, c), of_s.at[gi, c])
                wait_for(x_piece(0, c), xf_s.at[mirrored(v, 0), c])
                if c == 1:
                    wait_for(x_piece(0, c), xi_s.at[mirrored(v, 0), c])

    each(sent)

    def sent_exchange(inv):
        wait_for(rows.at[inv, :, :, core], c_s.at[inv])
        wait_for(part.at[inv, :, :, pl.ds(0, 15)], k_s.at[inv])

    wait_for(rows.at[0, :, pl.ds(0, 15), 0], f_s.at[0])
    sent_exchange(0)

    @pl.when(edge)
    def _():
        sent_exchange(1)
        wait_for(nall.at[other, :, :, pl.ds(0, 15)], g_s)

    @pl.when(~edge)
    def _():
        wait_for(rows.at[1, :, :, 0], f_s.at[1])

    wait_for(coef.at[:, pl.ds(0, 15)], ip_s)

    @pl.when((s == 0) | (s == 3))
    def _():
        wait_for(coef.at[:, 0], iz_s)


def on_device(normal_ops, integrals, site_terms, basis):
    inputs = (normal_ops.reshape(2, 2, 16, 8, 128), integrals, site_terms, basis)
    shapes = (
        jax.ShapeDtypeStruct((2, 2, 4, 128, 128), F32),
        jax.ShapeDtypeStruct((2, 1, 4, 128, 128), F32),
    )
    sem = pltpu.SemaphoreType.DMA
    vmem = pl.BlockSpec(memory_space=pltpu.VMEM)
    return pl.pallas_call(
        kernel,
        name="renormalize",
        out_shape=shapes,
        in_specs=[pl.BlockSpec(memory_space=pltpu.HBM)] * 4,
        out_specs=(vmem, vmem),
        scratch_shapes=[
            pltpu.VMEM((2, 1, 128), F32),
            pltpu.SMEM((2, 1, 4, 4), F32),
            pltpu.VMEM((2, 4, 512, 128), F32),
            pltpu.VMEM((4, 768, 512), BF16),
            pltpu.VMEM((4, 2, 2, 16, 8, 128), F32),
            pltpu.VMEM((2, 2, 16, 2, 2, 8, 128), F32),
            pltpu.VMEM((2, 16, 8, 128), F32),
            pltpu.VMEM((2, 2, 2, 16, 8, 128), F32),
            pltpu.VMEM((2, 2, 2, 16, 8, 128), F32),
            pltpu.VMEM((2, 2, 16, 8, 128), F32),
            pltpu.VMEM((4, 2, 16, 8, 128), F32),
            sem((4,)),
            sem((2, 3, 2)), sem((2, 3, 2)),
            sem, sem,
            sem((2,)), sem((2,)),
            sem((2,)), sem((2,)),
            sem, sem, sem, sem,
            sem((2,)), sem((2,)),
            sem((2,)), sem((2,)), sem((2,)), sem((2, 2)), sem((2, 2)),
            sem((2, 2)), sem((2, 2)), sem((4, 2)), sem((4, 2)), sem((4, 2)),
            pltpu.SemaphoreType.REGULAR,
        ],
        compiler_params=pltpu.CompilerParams(
            collective_id=0, has_side_effects=True, vmem_limit_bytes=32 * 2**20
        ),
    )(*(pltpu.with_memory_space_constraint(x, pltpu.HBM) for x in inputs))


def solution(mesh):
    placed = (
        P(None, "pair", None, "sec"),
        P(None, "pair", None),
        P(None, "pair", None, None),
        P(None, None, None, "sec"),
    )
    return jax.shard_map(
        on_device,
        mesh=mesh,
        in_specs=placed,
        out_specs=(P(None, "pair", None, None, "sec"), P(None, "pair", None, None, "sec")),
        check_vma=False,
    )
```
